256 devices in a mesh: grp: 2 (over core), seq: 16 (over y, z_hi), fsdp: 8 (over x, z_lo).
Axes of the slice: x: 4, y: 4, z: 8 (z_hi: 4, z_lo: 2; z = z_hi * 2 + z_lo), core: 2. Of those that a mesh axis runs over, the one named last changes fastest.
Arguments:
- new_rows: bfloat16 [2048, 5120], P('seq'), may hold values from -6 to 6
- cache_keys: bfloat16 [4, 1024, 3072], P(None, None, 'fsdp'), may hold values from -16 to 16
- cache_values: bfloat16 [4, 1024, 3072], P(None, None, 'fsdp'), may hold values from -6 to 6
- cache_frames: int32 [3], replicated, may hold values from 0 to 3
- real_bank: bfloat16 [2, 2048, 5120], P(None, 'seq'), may hold values from -6 to 6
- real_pick: int32 [2048], P('seq'), may hold values from 0 to 1
- attn_weights: bfloat16 [2, 3, 5120, 3072], P('grp', None, 'seq', 'fsdp'), may hold values from -1 to 1
- out_weights: bfloat16 [2, 3072, 5120], P('grp', 'seq', 'fsdp'), may hold values from -0.109375 to 0.109375
- norm_gains: float32 [2, 5120], P('grp'), may hold values from 0.5 to 1.5
- head_in: bfloat16 [5120, 128], P('fsdp'), may hold values from -0.078125 to 0.078125
- head_out: float32 [128], replicated, may hold values from -0.5 to 0.5
Outputs:
- wo_grads: bfloat16 [2, 3072, 5120], P('grp', 'seq', 'fsdp')
- losses: bfloat16 [2], P('grp')
The draws below stay inside these ranges and needn't reach their ends.
All inputs are finite; a program needn't handle non-finite values.
Results may differ from the reference program's by a relative error of at most 0.014.
The reference program's roundings to bfloat16 on the way (of `gen_heads`, `generated`, `gen_cot`, `head_grad` and `input_grad`) count: a program that leaves them out, or rounds other values in their place, can miss the bound.
Values may be sent and summed in bfloat16 or wider, within the bound.
No kernel may reach another device: no remote copies, remote signals or barrier semaphores. Data moves between devices by JAX's collectives and lax.ppermute only.
A program may use at most 128 MiB of HBM per device.

```python
import jax
import jax.numpy as jnp
from jax import lax

D = 5120
HEADS = 24
HD = 128
UNITS = 128
ROWS = 128
SINK = 1
WINDOW = 2
HIST = 4
BANK = 2
NEWTOK = 2048
FRAME = 1024
N_SEQ = 16
N_FSDP = 8


def planted_columns(key):
    head_key = jax.random.fold_in(key, 9101)
    chosen = jax.random.randint(jax.random.fold_in(head_key, 1), (), 0, HEADS)
    sign_vector = jnp.where(jax.random.bernoulli(jax.random.fold_in(head_key, 2), 0.5, (HD,)), 1.0, -1.0)
    magnitude = jax.random.uniform(jax.random.fold_in(head_key, 3), (HD,), jnp.float32, 0.5, 1.5)
    direction = sign_vector * magnitude
    column_head = jnp.arange(HEADS * HD) // HD
    return jnp.where(column_head == chosen, jnp.tile(direction, HEADS), 0.0)


def strength_factor(strength):
    return (strength / (1.083 * HD ** 0.5)) ** 0.5


def draw_attn_weights(key, part):
    spread = planted_columns(key)
    base = jax.random.truncated_normal(jax.random.fold_in(key, 9201), -4.0, 4.0, (2, 3, D, HEADS * HD), jnp.float32) * D ** (-0.5)
    row_sign = jnp.where(jax.random.bernoulli(jax.random.fold_in(key, 9202), 0.5, (2, 1, D, 1)), 1.0, -1.0)
    row_size = jax.random.uniform(jax.random.fold_in(key, 9203), (2, 1, D, 1), jnp.float32, 0.5, 1.5)
    factor = strength_factor(40.0)
    member_mask = jnp.array([1.0, 1.0, 0.0], jnp.float32).reshape(1, 3, 1, 1)
    planted = factor * row_sign * row_size * D ** (-0.5) * member_mask * spread
    return jnp.clip(base + planted, -1.0, 1.0).astype(jnp.bfloat16)


def draw_cache_keys(key, part):
    spread = planted_columns(key)
    base = jax.random.truncated_normal(jax.random.fold_in(key, 9301), -6.0, 6.0, (HIST, FRAME, HEADS * HD), jnp.float32)
    token_size = jax.random.normal(jax.random.fold_in(key, 9302), (HIST, FRAME, 1), jnp.float32)
    factor = strength_factor(40.0)
    return jnp.clip(base + factor * token_size * spread, -16.0, 16.0).astype(jnp.bfloat16)


def plant(entries, own_key, low, top_value):
    dims = entries.shape
    index_at = [jax.random.randint(jax.random.fold_in(own_key, axis), (), 0, dims[axis]) for axis in range(len(dims))]
    entries = entries.at[tuple(index_at)].set(low)
    longest = dims.index(max(dims))
    index_at[longest] = (index_at[longest] + 1) % dims[longest]
    return entries.at[tuple(index_at)].set(top_value)


def levels(own_key, dims, cuts, low, top_value):
    def one(position, blocks):
        draws = jax.random.uniform(jax.random.fold_in(jax.random.fold_in(own_key, 6), position), (blocks,), jnp.float32, low / len(cuts), top_value / len(cuts))
        return jnp.repeat(jnp.exp(draws), dims[position] // blocks).reshape((-1,) + (1,) * (len(dims) - position - 1))

    factor_of = one(*cuts[0])
    for cut in cuts[1:]:
        factor_of = factor_of * one(*cut)
    return factor_of


def bell_draw(stream_key, extent, deviation, limit, cuts=(), kind=jnp.bfloat16):
    level = levels(stream_key, extent, cuts, -0.22, 0.18) if cuts else 1.0
    result = jax.random.normal(stream_key, extent, jnp.float32) * deviation * level
    return jnp.minimum(jnp.maximum(result, -limit), limit).astype(kind)


def setup_inputs(seed: int = 0) -> dict:
    streams_of = jax.random.split(jax.random.key(seed), 12)
    new_rows = bell_draw(streams_of[0], (NEWTOK, D), 1.0, 6.0, ((0, 16),))
    cache_keys = draw_cache_keys(jax.random.fold_in(streams_of[11], 71), 0)
    cache_values = bell_draw(streams_of[2], (HIST, FRAME, HEADS * HD), 1.0, 6.0, ((2, 8),))
    cache_frames = jax.random.randint(streams_of[3], (SINK + WINDOW,), 0, HIST).astype(jnp.int32)
    real_bank = bell_draw(streams_of[4], (BANK, NEWTOK, D), 1.0, 6.0, ((1, 16),))
    real_pick = plant(jax.random.randint(streams_of[5], (NEWTOK,), 0, BANK), jax.random.fold_in(streams_of[5], 1), 0, BANK - 1).astype(jnp.int32)
    attn_weights = draw_attn_weights(jax.random.fold_in(streams_of[11], 71), 0)
    out_weights = bell_draw(streams_of[7], (2, HEADS * HD, D), (HEADS * HD) ** -0.5, 0.109375, ((0, 2), (1, 16), (2, 8)))
    norm_gains = jnp.clip(1.0 + 0.1 * jax.random.normal(streams_of[8], (2, D), jnp.float32), 0.5, 1.5)
    head_in = bell_draw(streams_of[9], (D, UNITS), D ** -0.5, 0.078125, ((0, 8),))
    head_out = bell_draw(streams_of[10], (UNITS,), UNITS ** -0.5, 0.5, (), jnp.float32)
    return {"new_rows": new_rows, "cache_keys": cache_keys, "cache_values": cache_values, "cache_frames": cache_frames, "real_bank": real_bank, "real_pick": real_pick, "attn_weights": attn_weights, "out_weights": out_weights, "norm_gains": norm_gains, "head_in": head_in, "head_out": head_out}


EPS = 1e-06
NEG = -1e+30

def rounded(value):
    return lax.optimization_barrier(value.astype(jnp.bfloat16)).astype(jnp.float32)

def project(row_block, gain_vector, weight_set):
    lifted = row_block.astype(jnp.float32)
    inverse = lax.rsqrt(lax.optimization_barrier(jnp.mean(lifted * lifted, axis=-1, keepdims=True)) + EPS)
    normed = (lifted * inverse * gain_vector).astype(jnp.bfloat16)
    projected = [jnp.dot(normed, weight_set[member], preferred_element_type=jnp.float32).astype(jnp.bfloat16) for member in range(3)]
    return (lifted, inverse, projected)

def split_heads(matrix):
    return matrix.reshape(matrix.shape[0], HEADS, HD).transpose(1, 0, 2)

def merge_heads(stacked):
    return stacked.transpose(1, 0, 2).reshape(stacked.shape[1], HEADS * HD)

def softmax_rows(queries, key_set, allowed):
    scores = jnp.dot(queries, key_set.T, preferred_element_type=jnp.float32) * HD ** (-0.5)
    scores = jnp.where(allowed, scores, NEG)
    row_max = lax.optimization_barrier(jnp.max(scores, axis=-1, keepdims=True))
    raised = jnp.exp(scores - row_max)
    return raised / lax.optimization_barrier(jnp.sum(raised, axis=-1, keepdims=True))

def attention(queries, key_set, value_set, allowed):

    def one_head(inputs):
        weights = softmax_rows(inputs[0], inputs[1], allowed)
        return jnp.dot(weights.astype(jnp.bfloat16), inputs[2], preferred_element_type=jnp.float32)
    stacked = lax.map(one_head, (split_heads(queries), split_heads(key_set), split_heads(value_set)))
    return merge_heads(stacked).astype(jnp.bfloat16)

def unit_direction(unit_values, head_out, head_in):
    _, gelu_back = jax.vjp(jax.nn.gelu, unit_values)
    unit_grad = gelu_back(jnp.broadcast_to(head_out, unit_values.shape))[0].astype(jnp.bfloat16)
    return jnp.dot(unit_grad, head_in.T, preferred_element_type=jnp.float32)

def block_grads(pairs):
    width = pairs[0][0].shape[1]
    total = jnp.zeros((width, D), jnp.float32)

    def step(block_index, carried):
        first_row = (block_index * ROWS).astype(jnp.int32)
        term = jnp.zeros((width, D), jnp.float32)
        for lead_heads, cotangent in pairs:
            lead_block = lax.dynamic_slice_in_dim(lead_heads, first_row, ROWS, 0)
            cot_block = lax.dynamic_slice_in_dim(cotangent, first_row, ROWS, 0)
            term = term + jnp.dot(lead_block.T, cot_block, preferred_element_type=jnp.float32)
        return carried + rounded(term)
    return lax.fori_loop(0, N_SEQ, step, total).astype(jnp.bfloat16)

def pick_rows(real_bank, real_pick):
    chosen = jnp.zeros(real_bank.shape[1:], real_bank.dtype)
    for entry in range(real_bank.shape[0]):
        chosen = jnp.where((real_pick == entry)[:, None], real_bank[entry], chosen)
    return chosen

def reference(new_rows, cache_keys, cache_values, cache_frames, real_bank, real_pick, attn_weights, out_weights, norm_gains, head_in, head_out):
    frame_len = NEWTOK // 2
    scale = HD ** (-0.5)
    _, _, (gen_q, gen_k, gen_v) = project(new_rows, norm_gains[0], attn_weights[0])
    picked_keys = cache_keys[cache_frames].reshape(-1, HEADS * HD)
    picked_values = cache_values[cache_frames].reshape(-1, HEADS * HD)
    token_frame = jnp.arange(NEWTOK) // frame_len
    gen_allowed = jnp.concatenate([jnp.ones((NEWTOK, picked_keys.shape[0]), jnp.bool_), token_frame[None, :] <= token_frame[:, None]], axis=1)
    gen_heads = attention(gen_q, jnp.concatenate([picked_keys, gen_k], axis=0), jnp.concatenate([picked_values, gen_v], axis=0), gen_allowed)
    generated = (new_rows.astype(jnp.float32) + jnp.dot(gen_heads, out_weights[0], preferred_element_type=jnp.float32)).astype(jnp.bfloat16)
    full_mask = jnp.ones((NEWTOK, NEWTOK), jnp.bool_)

    def critic(clip_rows):
        lifted, inverse, (crit_q, crit_k, crit_v) = project(clip_rows, norm_gains[1], attn_weights[1])
        heads = attention(crit_q, crit_k, crit_v, full_mask)
        outputs = (lifted + jnp.dot(heads, out_weights[1], preferred_element_type=jnp.float32)).astype(jnp.bfloat16)
        unit_values = jnp.dot(outputs, head_in, preferred_element_type=jnp.float32)
        return (lifted, inverse, crit_q, crit_k, crit_v, heads, unit_values)
    real_rows = pick_rows(real_bank, real_pick)
    _, _, _, _, _, real_heads, real_units = critic(real_rows)
    fake_lifted, fake_inverse, fake_q, fake_k, fake_v, fake_heads, fake_units = critic(generated)
    real_score = jnp.sum(jax.nn.gelu(real_units) * head_out)
    fake_score = jnp.sum(jax.nn.gelu(fake_units) * head_out)
    margin = (real_score - fake_score) / NEWTOK
    losses = jnp.stack([jax.nn.softplus(margin), jax.nn.softplus(-margin)]).astype(jnp.bfloat16)
    real_dir = unit_direction(real_units, head_out, head_in)
    fake_dir = unit_direction(fake_units, head_out, head_in)
    real_cot = (-jax.nn.sigmoid(-margin) * real_dir).astype(jnp.bfloat16)
    fake_cot = (jax.nn.sigmoid(-margin) * fake_dir).astype(jnp.bfloat16)
    gen_cot = (-jax.nn.sigmoid(margin) * fake_dir).astype(jnp.bfloat16)
    col_count = D // N_FSDP
    head_sum = jnp.zeros((NEWTOK, HEADS * HD), jnp.float32)
    for group_index in range(N_FSDP):
        low = group_index * col_count
        term = jnp.dot(gen_cot[:, low:low + col_count], out_weights[1][:, low:low + col_count].T, preferred_element_type=jnp.float32)
        head_sum = head_sum + rounded(term)
    head_grad = head_sum.astype(jnp.bfloat16)

    def head_back(inputs):
        queries, key_set, value_set, grad_out = inputs
        weights = softmax_rows(queries, key_set, full_mask)
        slopes = jnp.dot(grad_out, value_set.T, preferred_element_type=jnp.float32)
        score_grad = (weights * (slopes - lax.optimization_barrier(jnp.sum(slopes * weights, axis=-1, keepdims=True)))).astype(jnp.bfloat16)
        query_grad = jnp.dot(score_grad, key_set, preferred_element_type=jnp.float32) * scale
        score_blocks = score_grad.astype(jnp.float32).reshape(N_SEQ, ROWS, NEWTOK)
        query_blocks = queries.astype(jnp.float32).reshape(N_SEQ, ROWS, HD)
        key_parts = jnp.einsum('srk,srd->skd', score_blocks, query_blocks) * scale
        key_grad = lax.optimization_barrier(jnp.sum(rounded(key_parts), axis=0))
        weight_blocks = weights.astype(jnp.bfloat16).astype(jnp.float32).reshape(N_SEQ, ROWS, NEWTOK)
        grad_blocks = grad_out.astype(jnp.float32).reshape(N_SEQ, ROWS, HD)
        value_grad = lax.optimization_barrier(jnp.sum(rounded(jnp.einsum('srk,srd->skd', weight_blocks, grad_blocks)), axis=0))
        return (query_grad, key_grad, value_grad)
    query_g, key_g, value_g = lax.map(head_back, (split_heads(fake_q), split_heads(fake_k), split_heads(fake_v), split_heads(head_grad)))
    grads = [merge_heads(query_g).astype(jnp.bfloat16), merge_heads(key_g).astype(jnp.bfloat16), merge_heads(value_g).astype(jnp.bfloat16)]
    heads_per = HEADS * HD // N_FSDP
    row_grad = jnp.zeros((NEWTOK, D), jnp.float32)
    for group_index in range(N_FSDP):
        low = group_index * heads_per
        term = jnp.zeros((NEWTOK, D), jnp.float32)
        for member in range(3):
            term = term + jnp.dot(grads[member][:, low:low + heads_per], attn_weights[1][member][:, low:low + heads_per].T, preferred_element_type=jnp.float32)
        row_grad = row_grad + rounded(term)
    lifted_grad = row_grad * norm_gains[1]
    input_grad = (fake_inverse * lifted_grad + gen_cot.astype(jnp.float32)).astype(jnp.bfloat16)
    gen_grad = block_grads([(gen_heads, input_grad)])
    crit_grad = block_grads([(real_heads, real_cot), (fake_heads, fake_cot)])
    return (jnp.stack([gen_grad, crit_grad]), losses)
```

```python
import jax
import jax.numpy as jnp
from jax import lax
from jax.experimental import pallas as pl
from jax.experimental.pallas import tpu as pltpu
from jax.sharding import PartitionSpec as P

HD = 128
EPS = 1e-06
NEG = -1e30
AXES = ("grp", "seq", "fsdp")
VMEM = pltpu.CompilerParams(vmem_limit_bytes=50 * 2**20)
F32, BF16 = jnp.float32, jnp.bfloat16


def moved(value, step, groups=(0, 1), cross=False):
    dy, dz, dx, dw = step
    pairs = []
    for g in groups:
        for y in range(4):
            for z in range(4):
                for x in range(4):
                    for w in range(2):
                        there = 1 - g if cross else g
                        source = g * 128 + (4 * y + z) * 8 + 2 * x + w
                        target = (
                            there * 128
                            + (4 * ((y + dy) % 4) + (z + dz) % 4) * 8
                            + 2 * ((x + dx) % 4)
                            + (w + dw) % 2
                        )
                        pairs.append((source, target))
    return lax.ppermute(value, AXES, pairs)


def along(axis, k):
    step = [0, 0, 0, 0]
    step[axis] = k
    return tuple(step)


def ring4(value, axis, groups):
    one = moved(value, along(axis, 1), groups)
    three = moved(value, along(axis, -1), groups)
    cut = value.ndim - 2
    half = value.shape[cut] // 2
    low = lax.slice_in_dim(one, 0, half, axis=cut)
    high = lax.slice_in_dim(three, half, 2 * half, axis=cut)
    low = moved(low, along(axis, 1), groups)
    high = moved(high, along(axis, -1), groups)
    return jnp.stack([value, one, jnp.concatenate([low, high], axis=cut), three])


def direct4(value, axis, groups):
    return jnp.stack([value] + [moved(value, along(axis, k), groups) for k in (1, 2, 3)])


def gather_seq(value, groups, step=ring4):
    return step(step(value, 1, groups), 0, groups).reshape((4, 4) + value.shape)


def gather_fsdp(value, groups):
    pair = jnp.stack([value, moved(value, along(3, 1), groups)])
    return direct4(pair, 2, groups)


def swap_seq(blocks, groups):
    rows = [blocks[0]] + [moved(blocks[k], along(0, k), groups) for k in (1, 2, 3)]
    rows = jnp.stack(rows)
    cols = [rows[:, 0]] + [moved(rows[:, k], along(1, k), groups) for k in (1, 2, 3)]
    return jnp.stack(cols, axis=1)


def scatter_fsdp(blocks, groups):
    total = blocks[0].astype(F32)
    for k in (2, 1, 3):
        total = total + moved(blocks[k], along(2, k), groups).astype(F32)
    return total[0] + moved(total[1], along(3, 1), groups)


def ordered(relative, x, w):
    backward = jnp.stack([relative[k] for k in (0, 3, 2, 1)])
    return jnp.roll(backward, (x, w), (0, 1))


def mm(a, b, ca, cb):
    return lax.dot_general(a, b, (((ca,), (cb,)), ((), ())), preferred_element_type=F32)


def generator_kernel(frames, mask, q, k0, k1, k2, v0, v1, v2, own_k, own_v, out):
    scale = HD ** (-0.5)
    query = q[...]
    parts = [mm(query, k[0], 1, 1) * scale for k in (k0, k1, k2)]
    own = mm(query, own_k[...], 1, 1) * scale
    parts.append(jnp.where(mask[0:1, :] > 0.5, own, NEG))
    top = parts[0].max(axis=-1, keepdims=True)
    for part in parts[1:]:
        top = jnp.maximum(top, part.max(axis=-1, keepdims=True))
    parts = [jnp.exp(part - top) for part in parts]
    total = sum(part.sum(axis=-1, keepdims=True) for part in parts)
    inverse = 1.0 / total
    values = [v0[0], v1[0], v2[0], own_v[...]]
    result = jnp.zeros(out.shape, F32)
    for part, value in zip(parts, values):
        result = result + mm((part * inverse).astype(BF16), value, 1, 0)
    out[...] = result.astype(BF16)


def generator_attention(frames, mask, query, cache_keys, cache_values, key_value):
    rows, width = query.shape
    heads = width // HD
    count, length = key_value.shape[0], cache_keys.shape[1]

    def picked(i):
        return pl.BlockSpec((1, length, HD), lambda h, f: (f[i], 0, h))

    return pl.pallas_call(
        generator_kernel,
        grid_spec=pltpu.PrefetchScalarGridSpec(
            num_scalar_prefetch=1,
            grid=(heads,),
            in_specs=[
                pl.BlockSpec(mask.shape, lambda h, f: (0, 0)),
                pl.BlockSpec((rows, HD), lambda h, f: (0, h)),
                picked(0),
                picked(1),
                picked(2),
                picked(0),
                picked(1),
                picked(2),
                pl.BlockSpec((count, HD), lambda h, f: (0, h)),
                pl.BlockSpec((count, HD), lambda h, f: (0, heads + h)),
            ],
            out_specs=pl.BlockSpec((rows, HD), lambda h, f: (0, h)),
        ),
        out_shape=jax.ShapeDtypeStruct((rows, width), BF16),
        compiler_params=VMEM,
    )(
        frames, mask, query,
        cache_keys, cache_keys, cache_keys,
        cache_values, cache_values, cache_values,
        key_value, key_value,
    )


def critic_kernel(q, k, v, out, lse):
    scores = mm(q[...], k[...], 1, 1) * HD ** (-0.5)
    top = scores.max(axis=-1, keepdims=True)
    raised = jnp.exp(scores - top)
    total = raised.sum(axis=-1, keepdims=True)
    out[...] = mm((raised * (1.0 / total)).astype(BF16), v[...], 1, 0).astype(BF16)
    lse[...] = jnp.broadcast_to(top + jnp.log(total), lse.shape)


def critic_attention(query, key_value):
    rows, width = query.shape
    heads, count = width // HD, key_value.shape[0]
    own = pl.BlockSpec((rows, HD), lambda h: (0, h))
    return pl.pallas_call(
        critic_kernel,
        grid=(heads,),
        in_specs=[
            own,
            pl.BlockSpec((count, HD), lambda h: (0, h)),
            pl.BlockSpec((count, HD), lambda h: (0, heads + h)),
        ],
        out_specs=(own, own),
        out_shape=(
            jax.ShapeDtypeStruct((rows, width), BF16),
            jax.ShapeDtypeStruct((rows, width), F32),
        ),
        compiler_params=VMEM,
    )(query, key_value, key_value)


def query_kernel(q, kv, lse, u, high, low, score, grad, sent):
    scale = HD ** (-0.5)
    width = q.shape[1]
    unit = u[...]
    stats = []
    for start in range(0, width, HD):
        here = slice(start, start + HD)
        keys = kv[:, here]
        head_grad = (mm(unit, high[here, :], 1, 1) + mm(unit, low[here, :], 1, 1)).astype(BF16)
        logs = lse[:, start : start + 1]
        weights = jnp.exp(mm(q[:, here], keys, 1, 1) * scale - logs)
        slopes = mm(head_grad, kv[:, width + start : width + start + HD], 1, 1)
        centred = jnp.sum(slopes * weights, axis=-1, keepdims=True)
        score_grad = (weights * (slopes - centred)).astype(BF16)
        grad[:, here] = (mm(score_grad, keys, 1, 0) * scale).astype(BF16)
        stats += [centred, logs]
    stats.append(score[...])
    lane = lax.broadcasted_iota(jnp.int32, (q.shape[0], HD), 1)
    table = jnp.zeros((q.shape[0], HD), F32)
    for i, stat in enumerate(stats):
        for j in range(3):
            term = stat.astype(BF16).astype(F32)
            table = jnp.where(lane == 3 * i + j, term, table)
            stat = stat - term
    sent[:, :HD] = unit
    sent[:, HD:] = table.astype(BF16)


def query_grads(query, key_value, lse, unit, high, low, score):
    rows, width = query.shape
    return pl.pallas_call(
        query_kernel,
        out_shape=(
            jax.ShapeDtypeStruct((rows, width), BF16),
            jax.ShapeDtypeStruct((rows, 2 * HD), BF16),
        ),
        compiler_params=VMEM,
    )(query, key_value, lse, unit, high, low, score)


def key_kernel(k, v, q, sent, high, low, key_grad, value_grad):
    scale = HD ** (-0.5)
    width = k.shape[1]
    unit = sent[:, :HD]
    table = sent[:, HD:].astype(F32)

    def stat(i):
        return table[:, 3 * i : 3 * i + 1] + table[:, 3 * i + 1 : 3 * i + 2] + table[:, 3 * i + 2 : 3 * i + 3]

    for head, start in enumerate(range(0, width, HD)):
        here = slice(start, start + HD)
        queries = q[:, here]
        head_grad = (mm(unit, high[here, :], 1, 1) + mm(unit, low[here, :], 1, 1)).astype(BF16)
        weights = jnp.exp(mm(queries, k[:, here], 1, 1) * scale - stat(2 * head + 1))
        slopes = mm(head_grad, v[:, here], 1, 1)
        score_grad = (weights * (slopes - stat(2 * head))).astype(BF16)
        key_grad[:, here] = (mm(score_grad, queries, 0, 0) * scale).astype(BF16)
        value_grad[:, here] = mm(weights.astype(BF16), head_grad, 0, 0).astype(BF16)


def key_grads(keys, values, queries, sent, high, low):
    shape = jax.ShapeDtypeStruct(keys.shape, BF16)
    return pl.pallas_call(key_kernel, out_shape=(shape, shape), compiler_params=VMEM)(
        keys, values, queries, sent, high, low
    )


def split(value):
    high = lax.reduce_precision(value, 8, 7)
    return high.astype(BF16), (value - high).astype(BF16)


def project(row_block, gain_vector, weight_set):
    lifted = row_block.astype(F32)
    inverse = lax.rsqrt(jnp.mean(lifted * lifted, axis=-1, keepdims=True) + EPS)
    normed = (lifted * inverse * gain_vector).astype(BF16)
    parts = [jnp.dot(normed, weight_set[c], preferred_element_type=F32) for c in range(3)]
    return [part.astype(BF16) for part in parts], inverse


def unit_terms(units, head_out):
    active, back = jax.vjp(jax.nn.gelu, units)
    score = jnp.sum(active * head_out, axis=-1, keepdims=True)
    return score, back(jnp.broadcast_to(head_out, units.shape))[0].astype(BF16)


def pick_rows(real_bank, real_pick):
    chosen = jnp.zeros(real_bank.shape[1:], real_bank.dtype)
    for entry in range(real_bank.shape[0]):
        chosen = jnp.where((real_pick == entry)[:, None], real_bank[entry], chosen)
    return chosen


GEN, CRIT = (0,), (1,)


def local(
    new_rows, cache_keys, cache_values, cache_frames, real_bank, real_pick,
    attn_weights, out_weights, norm_gains, head_in, head_out,
):
    is_gen = lax.axis_index("grp") == 0
    seq_at, fsdp_at = lax.axis_index("seq"), lax.axis_index("fsdp")
    y, z, x, w = seq_at // 4, seq_at % 4, fsdp_at // 2, fsdp_at % 2
    rows, model = new_rows.shape
    cols = out_weights.shape[2]
    width = attn_weights.shape[3]
    tokens = rows * 16
    gains = norm_gains[0]
    start = fsdp_at * cols

    weights = lax.all_gather(attn_weights[0], "seq", axis=1, tiled=True)
    full_out = lax.all_gather(out_weights[0], "seq", axis=0, tiled=True)

    real_rows = pick_rows(real_bank, real_pick)
    first_rows = jnp.where(is_gen, new_rows, real_rows)
    (first_q, first_k, first_v), _ = project(first_rows, gains, weights)
    first_kv = gather_seq(jnp.concatenate([first_k, first_v], axis=1), (0, 1))
    first_kv = first_kv.reshape(tokens, 2 * width)
    key_y = (y - jnp.arange(tokens) // (4 * rows)) % 4
    mask = jnp.broadcast_to((key_y // 2 <= y // 2).astype(F32)[None], (8, tokens))
    first_heads = lax.cond(
        is_gen,
        lambda a: generator_attention(*a),
        lambda a: critic_attention(a[2], a[5])[0],
        (cache_frames, mask, first_q, cache_keys, cache_values, first_kv),
    )

    gathered = ordered(gather_fsdp(first_heads, GEN), x, w).reshape(8, rows, width)
    first_all = gathered.transpose(1, 0, 2).reshape(rows, 8 * width)
    first_cols = lax.dynamic_slice_in_dim(first_rows, start, cols, 1).astype(F32)
    generated = (first_cols + jnp.dot(first_all, full_out, preferred_element_type=F32)).astype(BF16)
    pair = jnp.stack([generated, moved(generated, along(3, 1), GEN)])
    crossed = jnp.stack([moved(pair, along(2, k), GEN, cross=True) for k in range(4)])
    crossed = ordered(crossed, x, w).reshape(8, rows, cols)
    second_rows = crossed.transpose(1, 0, 2).reshape(rows, model)

    to_seq = first_all.reshape(rows, 4, 4, 192).transpose(1, 2, 0, 3)
    gen_heads = swap_seq(jnp.roll(to_seq, (-y, -z), (0, 1)), GEN).reshape(tokens, 192)

    joint = jnp.dot(full_out, head_in, preferred_element_type=F32).reshape(4, 2, width, -1)
    joint = scatter_fsdp(jnp.roll(joint, (-x, -w), (0, 1)), CRIT)
    high, low = split(joint)

    def units_of(row_cols, heads):
        part = jnp.dot(row_cols, head_in, preferred_element_type=F32)
        part = part + jnp.dot(heads, high, preferred_element_type=F32)
        part = part + jnp.dot(heads, low, preferred_element_type=F32)
        return jnp.sum(gather_fsdp(part, CRIT), axis=(0, 1))

    real_cols = lax.dynamic_slice_in_dim(first_rows, start, cols, 1)
    real_score, real_unit = unit_terms(units_of(real_cols, first_heads), head_out)

    (second_q, second_k, second_v), inverse = project(second_rows, gains, weights)
    every = gather_seq(jnp.concatenate([second_k, second_v, second_q], axis=1), CRIT)
    every = every.reshape(tokens, 3 * width)
    second_heads, lse = critic_attention(second_q, every)
    second_cols = lax.dynamic_slice_in_dim(second_rows, start, cols, 1)
    fake_score, fake_unit = unit_terms(units_of(second_cols, second_heads), head_out)
    query_grad, sent = query_grads(
        second_q, every, lse, fake_unit, high, low, real_score - fake_score
    )
    sent = gather_seq(sent, CRIT, direct4).reshape(tokens, 2 * HD)
    key_grad, value_grad = key_grads(
        second_k, second_v, every[:, 2 * width :], sent, high, low
    )
    row_terms = sum(
        mm(grad, weights[c], 1, 1) for c, grad in enumerate((query_grad, key_grad, value_grad))
    ).astype(BF16)
    blocks = row_terms.reshape(rows, 4, 2, cols).transpose(1, 2, 0, 3)
    row_grad = scatter_fsdp(jnp.roll(blocks, (-x, -w), (0, 1)), CRIT)
    gain_cols = lax.dynamic_slice_in_dim(gains, start, cols, 0)
    direction = mm(fake_unit, head_in, 1, 1)
    input_grad = (inverse * row_grad * gain_cols + direction).astype(BF16)

    four = ring4(input_grad, 1, CRIT)
    back = jnp.stack([moved(four, along(0, k), CRIT, cross=True) for k in range(4)])
    back = back.reshape(tokens, cols)
    term_gen = mm(gen_heads, back, 0, 0)

    product = mm(second_heads, fake_unit, 0, 0) - mm(first_heads, real_unit, 0, 0)
    product = ordered(gather_fsdp(product.astype(BF16), CRIT), x, w).reshape(4, 4, 192, -1)
    product = swap_seq(jnp.roll(product, (-y, -z), (0, 1)), CRIT)
    product_high, product_low = split(jnp.sum(product.astype(F32), axis=(0, 1)))
    term_crit = mm(product_high, head_in, 1, 1) + mm(product_low, head_in, 1, 1)

    stats = sent[:, HD:].astype(F32)
    margin = jnp.sum(stats[:, 18:21]) / tokens
    margin_back = moved(jnp.broadcast_to(margin, (8, HD)), (0, 0, 0, 0), CRIT, cross=True)[0, 0]
    margin = jnp.where(is_gen, margin_back, margin)
    signed = jnp.where(is_gen, margin, -margin)
    factor = jnp.where(is_gen, -1.0, 1.0) * jax.nn.sigmoid(signed)
    grads = (jnp.where(is_gen, term_gen, term_crit) * factor).astype(BF16)
    losses = jax.nn.softplus(signed).astype(BF16)
    return (grads[None], losses[None])


def solution(mesh):
    placed = (
        P("seq", None),
        P(None, None, "fsdp"),
        P(None, None, "fsdp"),
        P(),
        P(None, "seq", None),
        P("seq"),
        P("grp", None, "seq", "fsdp"),
        P("grp", "seq", "fsdp"),
        P("grp", None),
        P("fsdp", None),
        P(),
    )
    return jax.shard_map(
        local,
        mesh=mesh,
        in_specs=placed,
        out_specs=(P("grp", "seq", "fsdp"), P("grp")),
        check_vma=False,
    )
```

```python
import jax
import jax.numpy as jnp
from jax import lax
from jax.experimental import pallas as pl
from jax.experimental.pallas import tpu as pltpu
from jax.sharding import PartitionSpec as P

HD = 128
EPS = 1e-06
NEG = -1e30
AXES = ("grp", "seq", "fsdp")
VMEM = pltpu.CompilerParams(vmem_limit_bytes=50 * 2**20)
F32, BF16 = jnp.float32, jnp.bfloat16


def moved(value, step, groups=(0, 1), cross=False):
    dy, dz, dx, dw = step
    pairs = []
    for g in groups:
        for y in range(4):
            for z in range(4):
                for x in range(4):
                    for w in range(2):
                        there = 1 - g if cross else g
                        source = g * 128 + (4 * y + z) * 8 + 2 * x + w
                        target = (
                            there * 128
                            + (4 * ((y + dy) % 4) + (z + dz) % 4) * 8
                            + 2 * ((x + dx) % 4)
                            + (w + dw) % 2
                        )
                        pairs.append((source, target))
    return lax.ppermute(value, AXES, pairs)


def along(axis, k):
    step = [0, 0, 0, 0]
    step[axis] = k
    return tuple(step)


def ring4(value, axis, groups):
    one = moved(value, along(axis, 1), groups)
    three = moved(value, along(axis, -1), groups)
    cut = value.ndim - 2
    half = value.shape[cut] // 2
    low = lax.slice_in_dim(one, 0, half, axis=cut)
    high = lax.slice_in_dim(three, half, 2 * half, axis=cut)
    low = moved(low, along(axis, 1), groups)
    high = moved(high, along(axis, -1), groups)
    return jnp.stack([value, one, jnp.concatenate([low, high], axis=cut), three])


def direct4(value, axis, groups):
    return jnp.stack([value] + [moved(value, along(axis, k), groups) for k in (1, 2, 3)])


def gather_seq(value, groups, step=ring4):
    return step(step(value, 1, groups), 0, groups).reshape((4, 4) + value.shape)


def gather_fsdp(value, groups, cross=False):
    parts = []
    for dx in range(4):
        for dw in range(2):
            stays = dx == dw == 0 and not cross
            parts.append(value if stays else moved(value, (0, 0, dx, dw), groups, cross))
    return jnp.stack(parts).reshape((4, 2) + value.shape)


def swap_seq(blocks, groups):
    rows = [blocks[0]] + [moved(blocks[k], along(0, k), groups) for k in (1, 2, 3)]
    rows = jnp.stack(rows)
    cols = [rows[:, 0]] + [moved(rows[:, k], along(1, k), groups) for k in (1, 2, 3)]
    return jnp.stack(cols, axis=1)


def scatter_fsdp(blocks, groups):
    total = blocks[0, 0].astype(F32)
    for dx in range(4):
        for dw in range(2):
            if dx or dw:
                total = total + moved(blocks[dx, dw], (0, 0, dx, dw), groups).astype(F32)
    return total


def after(value, other):
    first = other[(slice(0, 1),) * other.ndim].reshape(())
    return value + (first.astype(F32) * 0.0).astype(value.dtype)


def ring_parts(value, axis, groups):
    one = moved(value, along(axis, 1), groups)
    three = moved(value, along(axis, -1), groups)
    half = value.shape[0] // 2
    low = moved(one[:half], along(axis, 1), groups)
    high = moved(three[half:], along(axis, -1), groups)
    return [(0, 0, value), (1, 0, one), (3, 0, three), (2, 0, low), (2, half, high)]


def gather_weights(shard, groups, y, z):
    depth, width = shard.shape
    cut = 2 * width // 3
    part = shard[:, :cut]
    line = jnp.zeros((4, depth, cut), shard.dtype)
    for back, first, piece in ring_parts(part, 1, groups):
        line = lax.dynamic_update_slice(line, piece[None], ((z - back) % 4, first, 0))
    lead = jnp.zeros((4, 4, depth, cut), shard.dtype)
    for back, first, piece in ring_parts(line, 0, groups):
        lead = lax.dynamic_update_slice(lead, piece[None], ((y - back) % 4, first, 0, 0))
    part = shard[:, cut:]
    line = jnp.zeros((4, depth, width - cut), shard.dtype)
    for back, first, piece in ring_parts(part, 0, groups):
        line = lax.dynamic_update_slice(line, piece[None], ((y - back) % 4, first, 0))
    tail = jnp.zeros((4, 4, depth, width - cut), shard.dtype)
    for back, first, piece in ring_parts(line, 1, groups):
        tail = lax.dynamic_update_slice(tail, piece[:, None], (first, (z - back) % 4, 0, 0))
    return lead.reshape(16 * depth, cut), tail.reshape(16 * depth, width - cut)


def ordered(relative, x, w):
    backward = jnp.stack([relative[k] for k in (0, 3, 2, 1)])
    return jnp.roll(backward, (x, w), (0, 1))


def mm(a, b, ca, cb):
    return lax.dot_general(a, b, (((ca,), (cb,)), ((), ())), preferred_element_type=F32)


def generator_kernel(frames, mask, q, k0, k1, k2, v0, v1, v2, own_k, own_v, out):
    scale = HD ** (-0.5)
    query = q[...]
    parts = [mm(query, k[0], 1, 1) * scale for k in (k0, k1, k2)]
    own = mm(query, own_k[...], 1, 1) * scale
    parts.append(jnp.where(mask[0:1, :] > 0.5, own, NEG))
    top = parts[0].max(axis=-1, keepdims=True)
    for part in parts[1:]:
        top = jnp.maximum(top, part.max(axis=-1, keepdims=True))
    parts = [jnp.exp(part - top) for part in parts]
    total = sum(part.sum(axis=-1, keepdims=True) for part in parts)
    inverse = 1.0 / total
    values = [v0[0], v1[0], v2[0], own_v[...]]
    result = jnp.zeros(out.shape, F32)
    for part, value in zip(parts, values):
        result = result + mm((part * inverse).astype(BF16), value, 1, 0)
    out[...] = result.astype(BF16)


def generator_attention(frames, mask, query, cache_keys, cache_values, key_value):
    rows, width = query.shape
    heads = width // HD
    count, length = key_value.shape[0], cache_keys.shape[1]

    def picked(i):
        return pl.BlockSpec((1, length, HD), lambda h, f: (f[i], 0, h))

    return pl.pallas_call(
        generator_kernel,
        grid_spec=pltpu.PrefetchScalarGridSpec(
            num_scalar_prefetch=1,
            grid=(heads,),
            in_specs=[
                pl.BlockSpec(mask.shape, lambda h, f: (0, 0)),
                pl.BlockSpec((rows, HD), lambda h, f: (0, h)),
                picked(0),
                picked(1),
                picked(2),
                picked(0),
                picked(1),
                picked(2),
                pl.BlockSpec((count, HD), lambda h, f: (0, h)),
                pl.BlockSpec((count, HD), lambda h, f: (0, heads + h)),
            ],
            out_specs=pl.BlockSpec((rows, HD), lambda h, f: (0, h)),
        ),
        out_shape=jax.ShapeDtypeStruct((rows, width), BF16),
        compiler_params=VMEM,
    )(
        frames, mask, query,
        cache_keys, cache_keys, cache_keys,
        cache_values, cache_values, cache_values,
        key_value, key_value,
    )


def critic_kernel(q, k, v, out, lse):
    scores = mm(q[...], k[...], 1, 1) * HD ** (-0.5)
    top = scores.max(axis=-1, keepdims=True)
    raised = jnp.exp(scores - top)
    total = raised.sum(axis=-1, keepdims=True)
    out[...] = mm((raised * (1.0 / total)).astype(BF16), v[...], 1, 0).astype(BF16)
    lse[...] = jnp.broadcast_to(top + jnp.log(total), lse.shape)


def critic_attention(query, key_value):
    rows, width = query.shape
    heads, count = width // HD, key_value.shape[0]
    own = pl.BlockSpec((rows, HD), lambda h: (0, h))
    return pl.pallas_call(
        critic_kernel,
        grid=(heads,),
        in_specs=[
            own,
            pl.BlockSpec((count, HD), lambda h: (0, h)),
            pl.BlockSpec((count, HD), lambda h: (0, heads + h)),
        ],
        out_specs=(own, own),
        out_shape=(
            jax.ShapeDtypeStruct((rows, width), BF16),
            jax.ShapeDtypeStruct((rows, width), F32),
        ),
        compiler_params=VMEM,
    )(query, key_value, key_value)


def query_kernel(q, kv, lse, u, high, low, score, grad, sent):
    scale = HD ** (-0.5)
    width = q.shape[1]
    unit = u[...]
    stats = []
    for start in range(0, width, HD):
        here = slice(start, start + HD)
        keys = kv[:, here]
        head_grad = (mm(unit, high[here, :], 1, 1) + mm(unit, low[here, :], 1, 1)).astype(BF16)
        logs = lse[:, start : start + 1]
        weights = jnp.exp(mm(q[:, here], keys, 1, 1) * scale - logs)
        slopes = mm(head_grad, kv[:, width + start : width + start + HD], 1, 1)
        centred = jnp.sum(slopes * weights, axis=-1, keepdims=True)
        score_grad = (weights * (slopes - centred)).astype(BF16)
        grad[:, here] = (mm(score_grad, keys, 1, 0) * scale).astype(BF16)
        stats += [centred, logs]
    stats.append(score[...])
    lane = lax.broadcasted_iota(jnp.int32, (q.shape[0], HD), 1)
    table = jnp.zeros((q.shape[0], HD), F32)
    for i, stat in enumerate(stats):
        for j in range(3):
            term = stat.astype(BF16).astype(F32)
            table = jnp.where(lane == 3 * i + j, term, table)
            stat = stat - term
    sent[:, :HD] = unit
    sent[:, HD:] = table.astype(BF16)


def query_grads(query, key_value, lse, unit, high, low, score):
    rows, width = query.shape
    return pl.pallas_call(
        query_kernel,
        out_shape=(
            jax.ShapeDtypeStruct((rows, width), BF16),
            jax.ShapeDtypeStruct((rows, 2 * HD), BF16),
        ),
        compiler_params=VMEM,
    )(query, key_value, lse, unit, high, low, score)


def key_kernel(k, v, q, sent, high, low, key_grad, value_grad):
    scale = HD ** (-0.5)
    width = k.shape[1]
    unit = sent[:, :HD]
    table = sent[:, HD:].astype(F32)

    def stat(i):
        return table[:, 3 * i : 3 * i + 1] + table[:, 3 * i + 1 : 3 * i + 2] + table[:, 3 * i + 2 : 3 * i + 3]

    for head, start in enumerate(range(0, width, HD)):
        here = slice(start, start + HD)
        queries = q[:, here]
        head_grad = (mm(unit, high[here, :], 1, 1) + mm(unit, low[here, :], 1, 1)).astype(BF16)
        weights = jnp.exp(mm(queries, k[:, here], 1, 1) * scale - stat(2 * head + 1))
        slopes = mm(head_grad, v[:, here], 1, 1)
        score_grad = (weights * (slopes - stat(2 * head))).astype(BF16)
        key_grad[:, here] = (mm(score_grad, queries, 0, 0) * scale).astype(BF16)
        value_grad[:, here] = mm(weights.astype(BF16), head_grad, 0, 0).astype(BF16)


def key_grads(keys, values, queries, sent, high, low):
    shape = jax.ShapeDtypeStruct(keys.shape, BF16)
    return pl.pallas_call(key_kernel, out_shape=(shape, shape), compiler_params=VMEM)(
        keys, values, queries, sent, high, low
    )


def split(value):
    high = lax.reduce_precision(value, 8, 7)
    return high.astype(BF16), (value - high).astype(BF16)


def project(row_block, gain_vector, weights):
    lead, tail = weights
    width = tail.shape[1]
    lifted = row_block.astype(F32)
    inverse = lax.rsqrt(jnp.mean(lifted * lifted, axis=-1, keepdims=True) + EPS)
    normed = (lifted * inverse * gain_vector).astype(BF16)
    pair = jnp.dot(normed, lead, preferred_element_type=F32).astype(BF16)
    values = jnp.dot(normed, tail, preferred_element_type=F32).astype(BF16)
    return (pair[:, :width], pair[:, width:], values), inverse


def unit_terms(units, head_out):
    active, back = jax.vjp(jax.nn.gelu, units)
    score = jnp.sum(active * head_out, axis=-1, keepdims=True)
    return score, back(jnp.broadcast_to(head_out, units.shape))[0].astype(BF16)


def pick_rows(real_bank, real_pick):
    chosen = jnp.zeros(real_bank.shape[1:], real_bank.dtype)
    for entry in range(real_bank.shape[0]):
        chosen = jnp.where((real_pick == entry)[:, None], real_bank[entry], chosen)
    return chosen


GEN, CRIT = (0,), (1,)


def local(
    new_rows, cache_keys, cache_values, cache_frames, real_bank, real_pick,
    attn_weights, out_weights, norm_gains, head_in, head_out,
):
    is_gen = lax.axis_index("grp") == 0
    seq_at, fsdp_at = lax.axis_index("seq"), lax.axis_index("fsdp")
    y, z, x, w = seq_at // 4, seq_at % 4, fsdp_at // 2, fsdp_at % 2
    rows, model = new_rows.shape
    cols = out_weights.shape[2]
    width = attn_weights.shape[3]
    tokens = rows * 16
    gains = norm_gains[0]
    start = fsdp_at * cols

    full_out = lax.all_gather(out_weights[0], "seq", axis=0, tiled=True)
    shard = jnp.concatenate([attn_weights[0, c] for c in range(3)], axis=1)
    gen_weights = gather_weights(shard, GEN, y, z)
    arrived = moved(gen_weights[0][:8, :HD] + gen_weights[1][:8, :HD], (0, 0, 0, 0), GEN, cross=True)
    weights = gather_weights(after(shard, arrived), CRIT, y, z)

    (first_q, first_k, first_v), _ = project(new_rows, gains, gen_weights)
    first_kv = gather_seq(jnp.concatenate([first_k, first_v], axis=1), GEN)
    first_kv = first_kv.reshape(tokens, 2 * width)
    key_y = (y - jnp.arange(tokens) // (4 * rows)) % 4
    mask = jnp.broadcast_to((key_y // 2 <= y // 2).astype(F32)[None], (8, tokens))
    first_heads = lax.cond(
        is_gen,
        lambda a: generator_attention(*a),
        lambda a: jnp.zeros_like(a[2]),
        (cache_frames, mask, first_q, cache_keys, cache_values, first_kv),
    )

    gathered = ordered(gather_fsdp(first_heads, GEN), x, w).reshape(8, rows, width)
    first_all = gathered.transpose(1, 0, 2).reshape(rows, 8 * width)
    first_cols = lax.dynamic_slice_in_dim(new_rows, start, cols, 1).astype(F32)
    generated = (first_cols + jnp.dot(first_all, full_out, preferred_element_type=F32)).astype(BF16)
    crossed = ordered(gather_fsdp(generated, GEN, cross=True), x, w).reshape(8, rows, cols)
    second_rows = crossed.transpose(1, 0, 2).reshape(rows, model)

    to_seq = after(first_all, generated).reshape(rows, 4, 4, 192).transpose(1, 2, 0, 3)
    gen_heads = swap_seq(jnp.roll(to_seq, (-y, -z), (0, 1)), GEN).reshape(tokens, 192)

    joint = jnp.dot(full_out, head_in, preferred_element_type=F32).reshape(4, 2, width, -1)
    joint = scatter_fsdp(jnp.roll(joint, (-x, -w), (0, 1)), CRIT)
    high, low = split(joint)

    def units_of(row_cols, heads):
        part = jnp.dot(row_cols, head_in, preferred_element_type=F32)
        part = part + jnp.dot(heads, high, preferred_element_type=F32)
        part = part + jnp.dot(heads, low, preferred_element_type=F32)
        return jnp.sum(gather_fsdp(part, CRIT), axis=(0, 1))

    real_rows = pick_rows(real_bank, real_pick)

    def real_project(operands):
        (real_q, real_k, real_v), _ = project(operands[0], operands[1], operands[2:])
        return real_q, jnp.concatenate([real_k, real_v], axis=1)

    real_q, real_kv = lax.cond(
        is_gen,
        lambda a: (jnp.zeros((rows, width), BF16), jnp.zeros((rows, 2 * width), BF16)),
        real_project,
        (real_rows, gains, *weights),
    )
    real_kv = gather_seq(real_kv, CRIT)
    real_heads = lax.cond(
        is_gen,
        lambda a: jnp.zeros_like(a[0]),
        lambda a: critic_attention(*a)[0],
        (real_q, real_kv.reshape(tokens, 2 * width)),
    )
    real_cols = lax.dynamic_slice_in_dim(real_rows, start, cols, 1)
    real_score, real_unit = unit_terms(units_of(real_cols, real_heads), head_out)

    (second_q, second_k, second_v), inverse = project(second_rows, gains, weights)
    every = gather_seq(jnp.concatenate([second_k, second_v, second_q], axis=1), CRIT)
    every = every.reshape(tokens, 3 * width)
    second_heads, lse = critic_attention(second_q, every)
    second_cols = lax.dynamic_slice_in_dim(second_rows, start, cols, 1)
    fake_score, fake_unit = unit_terms(units_of(second_cols, second_heads), head_out)
    query_grad, sent = query_grads(
        second_q, every, lse, fake_unit, high, low, real_score - fake_score
    )
    sent = gather_seq(sent, CRIT, direct4).reshape(tokens, 2 * HD)
    key_grad, value_grad = key_grads(
        second_k, second_v, every[:, 2 * width :], sent, high, low
    )
    lead, tail = weights
    lead_grads = jnp.concatenate([query_grad, key_grad], axis=1)
    row_terms = (mm(lead_grads, lead, 1, 1) + mm(value_grad, tail, 1, 1)).astype(BF16)
    blocks = row_terms.reshape(rows, 4, 2, cols).transpose(1, 2, 0, 3)
    row_grad = scatter_fsdp(jnp.roll(blocks, (-x, -w), (0, 1)), CRIT)
    gain_cols = lax.dynamic_slice_in_dim(gains, start, cols, 0)
    direction = mm(fake_unit, head_in, 1, 1)
    input_grad = (inverse * row_grad * gain_cols + direction).astype(BF16)

    four = direct4(input_grad, 1, CRIT)
    back = jnp.stack([moved(four, along(0, k), CRIT, cross=True) for k in range(4)])
    back = back.reshape(tokens, cols)
    term_gen = mm(gen_heads, back, 0, 0)

    product = mm(second_heads, fake_unit, 0, 0) - mm(real_heads, real_unit, 0, 0)
    product = moved(product.astype(BF16), (0, 0, 0, 0), CRIT, cross=True)
    product = ordered(gather_fsdp(product, GEN), x, w).reshape(4, 4, 192, -1)
    product = swap_seq(jnp.roll(product, (-y, -z), (0, 1)), GEN)
    product = jnp.sum(product.astype(F32), axis=(0, 1))
    product_high, product_low = split(moved(product, (0, 0, 0, 0), GEN, cross=True))
    term_crit = mm(product_high, head_in, 1, 1) + mm(product_low, head_in, 1, 1)

    stats = sent[:, HD:].astype(F32)
    margin = jnp.sum(stats[:, 18:21]) / tokens
    margin_back = moved(jnp.broadcast_to(margin, (8, HD)), (0, 0, 0, 0), CRIT, cross=True)[0, 0]
    margin = jnp.where(is_gen, margin_back, margin)
    signed = jnp.where(is_gen, margin, -margin)
    factor = jnp.where(is_gen, -1.0, 1.0) * jax.nn.sigmoid(signed)
    grads = (jnp.where(is_gen, term_gen, term_crit) * factor).astype(BF16)
    losses = jax.nn.softplus(signed).astype(BF16)
    return (grads[None], losses[None])


def solution(mesh):
    placed = (
        P("seq", None),
        P(None, None, "fsdp"),
        P(None, None, "fsdp"),
        P(),
        P(None, "seq", None),
        P("seq"),
        P("grp", None, "seq", "fsdp"),
        P("grp", "seq", "fsdp"),
        P("grp", None),
        P("fsdp", None),
        P(),
    )
    return jax.shard_map(
        local,
        mesh=mesh,
        in_specs=placed,
        out_specs=(P("grp", "seq", "fsdp"), P("grp")),
        check_vma=False,
    )
```

```python
import jax
import jax.numpy as jnp
from jax import lax
from jax.experimental import pallas as pl
from jax.experimental.pallas import tpu as pltpu
from jax.sharding import PartitionSpec as P

HD = 128
EPS = 1e-06
NEG = -1e30
AXES = ("grp", "seq", "fsdp")
VMEM = pltpu.CompilerParams(vmem_limit_bytes=50 * 2**20)
F32, BF16 = jnp.float32, jnp.bfloat16


def moved(value, step, groups=(0, 1), cross=False):
    dy, dz, dx, dw = step
    pairs = []
    for g in groups:
        for y in range(4):
            for z in range(4):
                for x in range(4):
                    for w in range(2):
                        there = 1 - g if cross else g
                        source = g * 128 + (4 * y + z) * 8 + 2 * x + w
                        target = (
                            there * 128
                            + (4 * ((y + dy) % 4) + (z + dz) % 4) * 8
                            + 2 * ((x + dx) % 4)
                            + (w + dw) % 2
                        )
                        pairs.append((source, target))
    return lax.ppermute(value, AXES, pairs)


def along(axis, k):
    step = [0, 0, 0, 0]
    step[axis] = k
    return tuple(step)


def direct4(value, axis, groups):
    return jnp.stack([value] + [moved(value, along(axis, k), groups) for k in (1, 2, 3)])


def gather_seq(value, groups):
    return direct4(direct4(value, 1, groups), 0, groups).reshape((4, 4) + value.shape)


def gather_fsdp(value, groups):
    pair = jnp.stack([value, moved(value, along(3, 1), groups)])
    return direct4(pair, 2, groups)


def swap_seq(blocks, groups):
    rows = [blocks[0]] + [moved(blocks[k], along(0, k), groups) for k in (1, 2, 3)]
    rows = jnp.stack(rows)
    cols = [rows[:, 0]] + [moved(rows[:, k], along(1, k), groups) for k in (1, 2, 3)]
    return jnp.stack(cols, axis=1)


def scatter_fsdp(blocks, groups):
    total = blocks[0].astype(F32)
    for k in (2, 1, 3):
        total = total + moved(blocks[k], along(2, k), groups).astype(F32)
    return total[0] + moved(total[1], along(3, 1), groups)


def across(value, groups):
    return moved(value, (0, 0, 0, 0), groups, cross=True)


def after(value, other):
    first = other[(slice(0, 1),) * other.ndim].reshape(())
    return value + (first.astype(F32) * 0.0).astype(value.dtype)


def ordered(relative, x, w):
    backward = jnp.stack([relative[k] for k in (0, 3, 2, 1)])
    return jnp.roll(backward, (x, w), (0, 1))


def mm(a, b, ca, cb):
    return lax.dot_general(a, b, (((ca,), (cb,)), ((), ())), preferred_element_type=F32)


def generator_kernel(frames, mask, q, k0, k1, k2, v0, v1, v2, own_k, own_v, out):
    scale = HD ** (-0.5)
    query = q[...]
    parts = [mm(query, k[0], 1, 1) * scale for k in (k0, k1, k2)]
    own = mm(query, own_k[...], 1, 1) * scale
    parts.append(jnp.where(mask[0:1, :] > 0.5, own, NEG))
    top = parts[0].max(axis=-1, keepdims=True)
    for part in parts[1:]:
        top = jnp.maximum(top, part.max(axis=-1, keepdims=True))
    parts = [jnp.exp(part - top) for part in parts]
    total = sum(part.sum(axis=-1, keepdims=True) for part in parts)
    inverse = 1.0 / total
    values = [v0[0], v1[0], v2[0], own_v[...]]
    result = jnp.zeros(out.shape, F32)
    for part, value in zip(parts, values):
        result = result + mm((part * inverse).astype(BF16), value, 1, 0)
    out[...] = result.astype(BF16)


def generator_attention(frames, mask, query, cache_keys, cache_values, key_value):
    rows, width = query.shape
    heads = width // HD
    count, length = key_value.shape[0], cache_keys.shape[1]

    def picked(i):
        return pl.BlockSpec((1, length, HD), lambda h, f: (f[i], 0, h))

    return pl.pallas_call(
        generator_kernel,
        grid_spec=pltpu.PrefetchScalarGridSpec(
            num_scalar_prefetch=1,
            grid=(heads,),
            in_specs=[
                pl.BlockSpec(mask.shape, lambda h, f: (0, 0)),
                pl.BlockSpec((rows, HD), lambda h, f: (0, h)),
                picked(0),
                picked(1),
                picked(2),
                picked(0),
                picked(1),
                picked(2),
                pl.BlockSpec((count, HD), lambda h, f: (0, h)),
                pl.BlockSpec((count, HD), lambda h, f: (0, heads + h)),
            ],
            out_specs=pl.BlockSpec((rows, HD), lambda h, f: (0, h)),
        ),
        out_shape=jax.ShapeDtypeStruct((rows, width), BF16),
        compiler_params=VMEM,
    )(
        frames, mask, query,
        cache_keys, cache_keys, cache_keys,
        cache_values, cache_values, cache_values,
        key_value, key_value,
    )


def critic_kernel(q, k, v, out, lse):
    scores = mm(q[...], k[...], 1, 1) * HD ** (-0.5)
    top = scores.max(axis=-1, keepdims=True)
    raised = jnp.exp(scores - top)
    total = raised.sum(axis=-1, keepdims=True)
    out[...] = mm((raised * (1.0 / total)).astype(BF16), v[...], 1, 0).astype(BF16)
    lse[...] = jnp.broadcast_to(top + jnp.log(total), lse.shape)


def critic_attention(query, key_value):
    rows, width = query.shape
    heads, count = width // HD, key_value.shape[0]
    own = pl.BlockSpec((rows, HD), lambda h: (0, h))
    return pl.pallas_call(
        critic_kernel,
        grid=(heads,),
        in_specs=[
            own,
            pl.BlockSpec((count, HD), lambda h: (0, h)),
            pl.BlockSpec((count, HD), lambda h: (0, heads + h)),
        ],
        out_specs=(own, own),
        out_shape=(
            jax.ShapeDtypeStruct((rows, width), BF16),
            jax.ShapeDtypeStruct((rows, width), F32),
        ),
        compiler_params=VMEM,
    )(query, key_value, key_value)


def query_kernel(q, kv, lse, u, high, low, score, grad, sent):
    scale = HD ** (-0.5)
    width = q.shape[1]
    unit = u[...]
    stats = []
    for start in range(0, width, HD):
        here = slice(start, start + HD)
        keys = kv[:, here]
        head_grad = (mm(unit, high[here, :], 1, 1) + mm(unit, low[here, :], 1, 1)).astype(BF16)
        logs = lse[:, start : start + 1]
        weights = jnp.exp(mm(q[:, here], keys, 1, 1) * scale - logs)
        slopes = mm(head_grad, kv[:, width + start : width + start + HD], 1, 1)
        centred = jnp.sum(slopes * weights, axis=-1, keepdims=True)
        score_grad = (weights * (slopes - centred)).astype(BF16)
        grad[:, here] = (mm(score_grad, keys, 1, 0) * scale).astype(BF16)
        stats += [centred, logs]
    stats.append(score[...])
    lane = lax.broadcasted_iota(jnp.int32, (q.shape[0], HD), 1)
    table = jnp.zeros((q.shape[0], HD), F32)
    for i, stat in enumerate(stats):
        for j in range(3):
            term = stat.astype(BF16).astype(F32)
            table = jnp.where(lane == 3 * i + j, term, table)
            stat = stat - term
    sent[:, :HD] = unit
    sent[:, HD:] = table.astype(BF16)


def query_grads(query, key_value, lse, unit, high, low, score):
    rows, width = query.shape
    return pl.pallas_call(
        query_kernel,
        out_shape=(
            jax.ShapeDtypeStruct((rows, width), BF16),
            jax.ShapeDtypeStruct((rows, 2 * HD), BF16),
        ),
        compiler_params=VMEM,
    )(query, key_value, lse, unit, high, low, score)


def key_kernel(k, v, q, sent, high, low, key_grad, value_grad):
    scale = HD ** (-0.5)
    width = k.shape[1]
    unit = sent[:, :HD]
    table = sent[:, HD:].astype(F32)

    def stat(i):
        return table[:, 3 * i : 3 * i + 1] + table[:, 3 * i + 1 : 3 * i + 2] + table[:, 3 * i + 2 : 3 * i + 3]

    for head, start in enumerate(range(0, width, HD)):
        here = slice(start, start + HD)
        queries = q[:, here]
        head_grad = (mm(unit, high[here, :], 1, 1) + mm(unit, low[here, :], 1, 1)).astype(BF16)
        weights = jnp.exp(mm(queries, k[:, here], 1, 1) * scale - stat(2 * head + 1))
        slopes = mm(head_grad, v[:, here], 1, 1)
        score_grad = (weights * (slopes - stat(2 * head))).astype(BF16)
        key_grad[:, here] = (mm(score_grad, queries, 0, 0) * scale).astype(BF16)
        value_grad[:, here] = mm(weights.astype(BF16), head_grad, 0, 0).astype(BF16)


def key_grads(keys, values, queries, sent, high, low):
    shape = jax.ShapeDtypeStruct(keys.shape, BF16)
    return pl.pallas_call(key_kernel, out_shape=(shape, shape), compiler_params=VMEM)(
        keys, values, queries, sent, high, low
    )


def split(value):
    high = lax.reduce_precision(value, 8, 7)
    return high.astype(BF16), (value - high).astype(BF16)


def normalised(row_block, gain_vector):
    lifted = row_block.astype(F32)
    inverse = lax.rsqrt(jnp.mean(lifted * lifted, axis=-1, keepdims=True) + EPS)
    return (lifted * inverse * gain_vector).astype(BF16), inverse


def times(a, b):
    return jnp.dot(a, b, preferred_element_type=F32).astype(BF16)


def unit_terms(units, head_out):
    active, back = jax.vjp(jax.nn.gelu, units)
    score = jnp.sum(active * head_out, axis=-1, keepdims=True)
    return score, back(jnp.broadcast_to(head_out, units.shape))[0].astype(BF16)


def pick_rows(real_bank, real_pick):
    chosen = jnp.zeros(real_bank.shape[1:], real_bank.dtype)
    for entry in range(real_bank.shape[0]):
        chosen = jnp.where((real_pick == entry)[:, None], real_bank[entry], chosen)
    return chosen


GEN, CRIT = (0,), (1,)


def local(
    new_rows, cache_keys, cache_values, cache_frames, real_bank, real_pick,
    attn_weights, out_weights, norm_gains, head_in, head_out,
):
    is_gen = lax.axis_index("grp") == 0
    seq_at, fsdp_at = lax.axis_index("seq"), lax.axis_index("fsdp")
    y, z, x, w = seq_at // 4, seq_at % 4, fsdp_at // 2, fsdp_at % 2
    rows, model = new_rows.shape
    cols = out_weights.shape[2]
    width = attn_weights.shape[3]
    tokens = rows * 16
    gains = norm_gains[0]
    start = fsdp_at * cols

    shard_q, shard_k, shard_v = (attn_weights[0, c] for c in range(3))
    shard_kv = jnp.concatenate([shard_k, shard_v], axis=1)
    weights_kv = lax.all_gather(shard_kv, "seq", axis=0, tiled=True)
    weights_q = lax.all_gather(shard_q, "seq", axis=0, tiled=True)
    full_out = lax.all_gather(out_weights[0], "seq", axis=0, tiled=True)

    real_rows = pick_rows(real_bank, real_pick)
    first_rows = jnp.where(is_gen, new_rows, real_rows)
    first_normed, _ = normalised(first_rows, gains)
    first_kv = gather_seq(times(first_normed, weights_kv), (0, 1))
    first_kv = first_kv.reshape(tokens, 2 * width)
    first_q = times(first_normed, weights_q)
    key_y = (y - jnp.arange(tokens) // (4 * rows)) % 4
    mask = jnp.broadcast_to((key_y // 2 <= y // 2).astype(F32)[None], (8, tokens))
    first_heads = lax.cond(
        is_gen,
        lambda a: generator_attention(*a),
        lambda a: critic_attention(a[2], a[5])[0],
        (cache_frames, mask, first_q, cache_keys, cache_values, first_kv),
    )

    gathered = ordered(gather_fsdp(first_heads, GEN), x, w).reshape(8, rows, width)
    first_all = gathered.transpose(1, 0, 2).reshape(rows, 8 * width)
    first_cols = lax.dynamic_slice_in_dim(first_rows, start, cols, 1).astype(F32)
    generated = (first_cols + jnp.dot(first_all, full_out, preferred_element_type=F32)).astype(BF16)
    crossed = ordered(gather_fsdp(across(generated, GEN), CRIT), x, w).reshape(8, rows, cols)
    second_rows = crossed.transpose(1, 0, 2).reshape(rows, model)

    to_seq = first_all.reshape(rows, 4, 4, 192).transpose(1, 2, 0, 3)
    gen_heads = swap_seq(jnp.roll(to_seq, (-y, -z), (0, 1)), GEN).reshape(tokens, 192)

    joint = jnp.dot(full_out, head_in, preferred_element_type=F32)
    high, low = split(lax.psum_scatter(joint, "fsdp", scatter_dimension=0, tiled=True))

    def units_of(row_cols, heads):
        part = jnp.dot(row_cols, head_in, preferred_element_type=F32)
        part = part + jnp.dot(heads, high, preferred_element_type=F32)
        return part + jnp.dot(heads, low, preferred_element_type=F32)

    real_cols = lax.dynamic_slice_in_dim(first_rows, start, cols, 1)

    second_normed, inverse = normalised(second_rows, gains)
    second_kv = times(second_normed, weights_kv)
    second_k, second_v = second_kv[:, :width], second_kv[:, width:]
    second_q = times(second_normed, weights_q)
    every = gather_seq(jnp.concatenate([second_kv, second_q], axis=1), CRIT)
    every = every.reshape(tokens, 3 * width)
    second_heads, lse = critic_attention(second_q, every)
    second_cols = lax.dynamic_slice_in_dim(second_rows, start, cols, 1)
    units = jnp.stack([units_of(real_cols, first_heads), units_of(second_cols, second_heads)])
    units = jnp.sum(gather_fsdp(units, CRIT), axis=(0, 1))
    real_score, real_unit = unit_terms(units[0], head_out)
    fake_score, fake_unit = unit_terms(units[1], head_out)
    query_grad, sent = query_grads(
        second_q, every, lse, fake_unit, high, low, real_score - fake_score
    )
    sent = gather_seq(sent, CRIT).reshape(tokens, 2 * HD)
    key_grad, value_grad = key_grads(
        second_k, second_v, every[:, 2 * width :], sent, high, low
    )
    pair_grads = jnp.concatenate([key_grad, value_grad], axis=1)
    row_terms = (mm(query_grad, weights_q, 1, 1) + mm(pair_grads, weights_kv, 1, 1)).astype(BF16)
    blocks = row_terms.reshape(rows, 4, 2, cols).transpose(1, 2, 0, 3)
    row_grad = scatter_fsdp(jnp.roll(blocks, (-x, -w), (0, 1)), CRIT)
    gain_cols = lax.dynamic_slice_in_dim(gains, start, cols, 0)
    direction = mm(fake_unit, head_in, 1, 1)
    input_grad = (inverse * row_grad * gain_cols + direction).astype(BF16)

    back = direct4(across(direct4(input_grad, 1, CRIT), CRIT), 0, GEN)
    back = back.reshape(tokens, cols)
    term_gen = mm(gen_heads, back, 0, 0)

    product = mm(second_heads, fake_unit, 0, 0) - mm(first_heads, real_unit, 0, 0)
    product = lax.all_gather(product, "fsdp", axis=0, tiled=True)
    product = lax.psum_scatter(product, "seq", scatter_dimension=0, tiled=True)
    product_high, product_low = split(product)
    term_crit = mm(product_high, head_in, 1, 1) + mm(product_low, head_in, 1, 1)

    stats = sent[:, HD:].astype(F32)
    margin = jnp.sum(stats[:, 18:21]) / tokens
    margin_back = across(jnp.broadcast_to(margin, (8, HD)), CRIT)[0, 0]
    margin = jnp.where(is_gen, margin_back, margin)
    signed = jnp.where(is_gen, margin, -margin)
    factor = jnp.where(is_gen, -1.0, 1.0) * jax.nn.sigmoid(signed)
    grads = (jnp.where(is_gen, term_gen, term_crit) * factor).astype(BF16)
    losses = jax.nn.softplus(signed).astype(BF16)
    return (grads[None], losses[None])


def solution(mesh):
    placed = (
        P("seq", None),
        P(None, None, "fsdp"),
        P(None, None, "fsdp"),
        P(),
        P(None, "seq", None),
        P("seq"),
        P("grp", None, "seq", "fsdp"),
        P("grp", "seq", "fsdp"),
        P("grp", None),
        P("fsdp", None),
        P(),
    )
    return jax.shard_map(
        local,
        mesh=mesh,
        in_specs=placed,
        out_specs=(P("grp", "seq", "fsdp"), P("grp")),
        check_vma=False,
    )
```

```python
import jax
import jax.numpy as jnp
from jax import lax
from jax.experimental import pallas as pl
from jax.experimental.pallas import tpu as pltpu
from jax.sharding import PartitionSpec as P

HD = 128
EPS = 1e-06
NEG = -1e30
AXES = ("grp", "seq", "fsdp")
VMEM = pltpu.CompilerParams(vmem_limit_bytes=50 * 2**20)
F32, BF16 = jnp.float32, jnp.bfloat16


def moved(value, step, groups=(0, 1), cross=False):
    dy, dz, dx, dw = step
    pairs = []
    for g in groups:
        for y in range(4):
            for z in range(4):
                for x in range(4):
                    for w in range(2):
                        there = 1 - g if cross else g
                        source = g * 128 + (4 * y + z) * 8 + 2 * x + w
                        target = (
                            there * 128
                            + (4 * ((y + dy) % 4) + (z + dz) % 4) * 8
                            + 2 * ((x + dx) % 4)
                            + (w + dw) % 2
                        )
                        pairs.append((source, target))
    return lax.ppermute(value, AXES, pairs)


def along(axis, k):
    step = [0, 0, 0, 0]
    step[axis] = k
    return tuple(step)


def direct4(value, axis, groups):
    return jnp.stack([value] + [moved(value, along(axis, k), groups) for k in (1, 2, 3)])


def gather_seq(lead, tail, groups):
    lead, tail = direct4(lead, 1, groups), direct4(tail, 0, groups)
    lead = direct4(lead, 0, groups)
    tail = jnp.stack([tail] + [moved(tail, along(1, k), groups) for k in (1, 2, 3)], axis=1)
    return [part.reshape((-1, part.shape[-1])) for part in (lead, tail)]


def spread(value, axis):
    count = lax.axis_size(axis)
    return lax.all_to_all(jnp.broadcast_to(value[None], (count,) + value.shape), axis, 0, 0)


def gather_fsdp(value, groups):
    pair = jnp.stack([value, moved(value, along(3, 1), groups)])
    return direct4(pair, 2, groups)


def swap_seq(blocks, groups):
    rows = [blocks[0]] + [moved(blocks[k], along(0, k), groups) for k in (1, 2, 3)]
    rows = jnp.stack(rows)
    cols = [rows[:, 0]] + [moved(rows[:, k], along(1, k), groups) for k in (1, 2, 3)]
    return jnp.stack(cols, axis=1)


def across(value, groups):
    return moved(value, (0, 0, 0, 0), groups, cross=True)


def after(value, other):
    first = other[(slice(0, 1),) * other.ndim].reshape(())
    return value + (first.astype(F32) * 0.0).astype(value.dtype)


def ordered(relative, x, w):
    backward = jnp.stack([relative[k] for k in (0, 3, 2, 1)])
    return jnp.roll(backward, (x, w), (0, 1))


def mm(a, b, ca, cb):
    return lax.dot_general(a, b, (((ca,), (cb,)), ((), ())), preferred_element_type=F32)


def generator_kernel(frames, mask, q, k0, k1, k2, v0, v1, v2, own_k, own_v, out):
    scale = HD ** (-0.5)
    query = q[...]
    parts = [mm(query, k[0], 1, 1) * scale for k in (k0, k1, k2)]
    own = mm(query, own_k[...], 1, 1) * scale
    parts.append(jnp.where(mask[0:1, :] > 0.5, own, NEG))
    top = parts[0].max(axis=-1, keepdims=True)
    for part in parts[1:]:
        top = jnp.maximum(top, part.max(axis=-1, keepdims=True))
    parts = [jnp.exp(part - top) for part in parts]
    total = sum(part.sum(axis=-1, keepdims=True) for part in parts)
    inverse = 1.0 / total
    values = [v0[0], v1[0], v2[0], own_v[...]]
    result = jnp.zeros(out.shape, F32)
    for part, value in zip(parts, values):
        result = result + mm((part * inverse).astype(BF16), value, 1, 0)
    out[...] = result.astype(BF16)


def generator_attention(frames, mask, query, cache_keys, cache_values, own_keys, own_values):
    rows, width = query.shape
    heads = width // HD
    count, length = own_keys.shape[0], cache_keys.shape[1]

    def picked(i):
        return pl.BlockSpec((1, length, HD), lambda h, f: (f[i], 0, h))

    return pl.pallas_call(
        generator_kernel,
        grid_spec=pltpu.PrefetchScalarGridSpec(
            num_scalar_prefetch=1,
            grid=(heads,),
            in_specs=[
                pl.BlockSpec(mask.shape, lambda h, f: (0, 0)),
                pl.BlockSpec((rows, HD), lambda h, f: (0, h)),
                picked(0),
                picked(1),
                picked(2),
                picked(0),
                picked(1),
                picked(2),
                pl.BlockSpec((count, HD), lambda h, f: (0, h)),
                pl.BlockSpec((count, HD), lambda h, f: (0, h)),
            ],
            out_specs=pl.BlockSpec((rows, HD), lambda h, f: (0, h)),
        ),
        out_shape=jax.ShapeDtypeStruct((rows, width), BF16),
        compiler_params=VMEM,
    )(
        frames, mask, query,
        cache_keys, cache_keys, cache_keys,
        cache_values, cache_values, cache_values,
        own_keys, own_values,
    )


def column(lead, tail, index):
    count = lead.shape[1] // HD
    ref, index = (lead, index) if index < count else (tail, index - count)
    return ref[:, index * HD : (index + 1) * HD]


def critic_kernel(q, lead, tail, out, lse):
    heads = q.shape[1] // HD
    for head in range(heads):
        here = slice(head * HD, (head + 1) * HD)
        scores = mm(q[:, here], column(lead, tail, head), 1, 1) * HD ** (-0.5)
        top = scores.max(axis=-1, keepdims=True)
        raised = jnp.exp(scores - top)
        total = raised.sum(axis=-1, keepdims=True)
        weights = (raised * (1.0 / total)).astype(BF16)
        out[:, here] = mm(weights, column(lead, tail, heads + head), 1, 0).astype(BF16)
        lse[:, here] = jnp.broadcast_to(top + jnp.log(total), (q.shape[0], HD))


def critic_attention(query, lead, tail):
    return pl.pallas_call(
        critic_kernel,
        out_shape=(
            jax.ShapeDtypeStruct(query.shape, BF16),
            jax.ShapeDtypeStruct(query.shape, F32),
        ),
        compiler_params=VMEM,
    )(query, lead, tail)


def query_kernel(q, lead, tail, lse, u, high, low, score, grad, sent):
    scale = HD ** (-0.5)
    width = q.shape[1]
    unit = u[...]
    stats = []
    for head, start in enumerate(range(0, width, HD)):
        here = slice(start, start + HD)
        keys = column(lead, tail, head)
        head_grad = (mm(unit, high[here, :], 1, 1) + mm(unit, low[here, :], 1, 1)).astype(BF16)
        logs = lse[:, start : start + 1]
        weights = jnp.exp(mm(q[:, here], keys, 1, 1) * scale - logs)
        slopes = mm(head_grad, column(lead, tail, width // HD + head), 1, 1)
        centred = jnp.sum(slopes * weights, axis=-1, keepdims=True)
        score_grad = (weights * (slopes - centred)).astype(BF16)
        grad[:, here] = (mm(score_grad, keys, 1, 0) * scale).astype(BF16)
        stats += [centred, logs]
    stats.append(score[...])
    lane = lax.broadcasted_iota(jnp.int32, (q.shape[0], HD), 1)
    table = jnp.zeros((q.shape[0], HD), F32)
    for i, stat in enumerate(stats):
        for j in range(3):
            term = stat.astype(BF16).astype(F32)
            table = jnp.where(lane == 3 * i + j, term, table)
            stat = stat - term
    sent[:, :HD] = unit
    sent[:, HD:] = table.astype(BF16)


def query_grads(query, lead, tail, lse, unit, high, low, score):
    rows, width = query.shape
    return pl.pallas_call(
        query_kernel,
        out_shape=(
            jax.ShapeDtypeStruct((rows, width), BF16),
            jax.ShapeDtypeStruct((rows, 2 * HD), BF16),
        ),
        compiler_params=VMEM,
    )(query, lead, tail, lse, unit, high, low, score)


def key_kernel(at, k, v, tail, sent, high, low, key_grad, value_grad, ordered_sent):
    scale = HD ** (-0.5)
    rows, width = k.shape
    y, z = at[0] // 4, at[0] % 4
    for dy in range(4):
        for dz in range(4):
            place = ((y + 4 - dy) % 4) * 4 + (z + 4 - dz) % 4
            block = (4 * dy + dz) * rows
            ordered_sent[block : block + rows, :] = sent[pl.ds(place, 1)][0]
    unit = ordered_sent[:, :HD]
    table = ordered_sent[:, HD:].astype(F32)

    def stat(i):
        return table[:, 3 * i : 3 * i + 1] + table[:, 3 * i + 1 : 3 * i + 2] + table[:, 3 * i + 2 : 3 * i + 3]

    first = tail.shape[1] - width
    for head, start in enumerate(range(0, width, HD)):
        here = slice(start, start + HD)
        queries = tail[:, first + start : first + start + HD]
        head_grad = (mm(unit, high[here, :], 1, 1) + mm(unit, low[here, :], 1, 1)).astype(BF16)
        weights = jnp.exp(mm(queries, k[:, here], 1, 1) * scale - stat(2 * head + 1))
        slopes = mm(head_grad, v[:, here], 1, 1)
        score_grad = (weights * (slopes - stat(2 * head))).astype(BF16)
        key_grad[:, here] = (mm(score_grad, queries, 0, 0) * scale).astype(BF16)
        value_grad[:, here] = mm(weights.astype(BF16), head_grad, 0, 0).astype(BF16)


def key_grads(at, keys, values, tail, sent, high, low):
    shape = jax.ShapeDtypeStruct(keys.shape, BF16)
    whole = pl.BlockSpec(memory_space=pltpu.VMEM)
    return pl.pallas_call(
        key_kernel,
        in_specs=[pl.BlockSpec(memory_space=pltpu.SMEM)] + [whole] * 6,
        out_shape=(shape, shape),
        scratch_shapes=[pltpu.VMEM((tail.shape[0], sent.shape[-1]), BF16)],
        compiler_params=VMEM,
    )(at, keys, values, tail, sent, high, low)


def split(value):
    high = lax.reduce_precision(value, 8, 7)
    return high.astype(BF16), (value - high).astype(BF16)


def normalised(row_block, gain_vector):
    lifted = row_block.astype(F32)
    inverse = lax.rsqrt(jnp.mean(lifted * lifted, axis=-1, keepdims=True) + EPS)
    return (lifted * inverse * gain_vector).astype(BF16), inverse


def times(a, b):
    return jnp.dot(a, b, preferred_element_type=F32).astype(BF16)


def unit_terms(units, head_out):
    active, back = jax.vjp(jax.nn.gelu, units)
    score = jnp.sum(active * head_out, axis=-1, keepdims=True)
    return score, back(jnp.broadcast_to(head_out, units.shape))[0].astype(BF16)


def pick_rows(real_bank, real_pick):
    chosen = jnp.zeros(real_bank.shape[1:], real_bank.dtype)
    for entry in range(real_bank.shape[0]):
        chosen = jnp.where((real_pick == entry)[:, None], real_bank[entry], chosen)
    return chosen


GEN, CRIT = (0,), (1,)


def local(
    new_rows, cache_keys, cache_values, cache_frames, real_bank, real_pick,
    attn_weights, out_weights, norm_gains, head_in, head_out,
):
    is_gen = lax.axis_index("grp") == 0
    seq_at, fsdp_at = lax.axis_index("seq"), lax.axis_index("fsdp")
    y, z, x, w = seq_at // 4, seq_at % 4, fsdp_at // 2, fsdp_at % 2
    rows, model = new_rows.shape
    cols = out_weights.shape[2]
    width = attn_weights.shape[3]
    tokens = rows * 16
    gains = norm_gains[0]
    start = fsdp_at * cols

    shard = jnp.concatenate([attn_weights[0, c] for c in range(3)], axis=1)
    weights = lax.all_gather(shard, "seq", axis=0, tiled=True)
    full_out = lax.all_gather(out_weights[0], "seq", axis=0, tiled=True)

    real_rows = pick_rows(real_bank, real_pick)
    first_rows = jnp.where(is_gen, new_rows, real_rows)
    first_normed, _ = normalised(first_rows, gains)
    first = times(first_normed, weights)
    first_q = first[:, :width]
    first_k, first_v = gather_seq(first[:, width : 2 * width], first[:, 2 * width :], (0, 1))
    key_y = (y - jnp.arange(tokens) // (4 * rows)) % 4
    mask = jnp.broadcast_to((key_y // 2 <= y // 2).astype(F32)[None], (8, tokens))
    first_heads = lax.cond(
        is_gen,
        lambda a: generator_attention(*a),
        lambda a: critic_attention(a[2], a[5], a[6])[0],
        (cache_frames, mask, first_q, cache_keys, cache_values, first_k, first_v),
    )

    first_all = spread(first_heads, "fsdp").transpose(1, 0, 2).reshape(rows, 8 * width)
    first_cols = lax.dynamic_slice_in_dim(first_rows, start, cols, 1).astype(F32)
    generated = (first_cols + jnp.dot(first_all, full_out, preferred_element_type=F32)).astype(BF16)
    crossed = spread(across(generated, GEN), "fsdp")
    second_rows = crossed.transpose(1, 0, 2).reshape(rows, model)

    to_seq = first_all.reshape(rows, 4, 4, 192).transpose(1, 2, 0, 3)
    gen_heads = swap_seq(jnp.roll(to_seq, (-y, -z), (0, 1)), GEN).reshape(tokens, 192)

    joint = jnp.dot(full_out, head_in, preferred_element_type=F32)
    high, low = split(lax.psum_scatter(joint, "fsdp", scatter_dimension=0, tiled=True))

    def units_of(row_cols, heads):
        part = jnp.dot(row_cols, head_in, preferred_element_type=F32)
        part = part + jnp.dot(heads, high, preferred_element_type=F32)
        return part + jnp.dot(heads, low, preferred_element_type=F32)

    real_cols = lax.dynamic_slice_in_dim(first_rows, start, cols, 1)

    second_normed, inverse = normalised(second_rows, gains)
    second = times(second_normed, weights)
    second_q, second_k, second_v = (second[:, c * width : (c + 1) * width] for c in range(3))
    cut = width - HD
    every_lead, every_tail = gather_seq(
        jnp.concatenate([second_k, second_v[:, :cut]], axis=1),
        jnp.concatenate([second_v[:, cut:], second_q], axis=1),
        CRIT,
    )
    second_heads, lse = critic_attention(second_q, every_lead, every_tail)
    second_cols = lax.dynamic_slice_in_dim(second_rows, start, cols, 1)
    units = jnp.stack([units_of(real_cols, first_heads), units_of(second_cols, second_heads)])
    units = jnp.sum(spread(units, "fsdp"), axis=0)
    real_score, real_unit = unit_terms(units[0], head_out)
    fake_score, fake_unit = unit_terms(units[1], head_out)
    query_grad, sent = query_grads(
        second_q, every_lead, every_tail, lse, fake_unit, high, low, real_score - fake_score
    )
    sent = spread(sent, "seq")
    at = jnp.reshape(seq_at, (1,)).astype(jnp.int32)
    key_grad, value_grad = key_grads(at, second_k, second_v, every_tail, sent, high, low)
    grads = jnp.concatenate([query_grad, key_grad, value_grad], axis=1)
    row_terms = jnp.einsum(
        "tk,bnk->btn", grads, weights.reshape(8, cols, 3 * width), preferred_element_type=F32
    )
    row_terms = lax.all_to_all(row_terms.astype(BF16), "fsdp", 0, 0)
    row_grad = jnp.sum(row_terms.astype(F32), axis=0)
    gain_cols = lax.dynamic_slice_in_dim(gains, start, cols, 0)
    direction = mm(fake_unit, head_in, 1, 1)
    input_grad = (inverse * row_grad * gain_cols + direction).astype(BF16)

    product = mm(second_heads, fake_unit, 0, 0) - mm(first_heads, real_unit, 0, 0)
    product = across(after(product.astype(BF16), gen_heads), CRIT)
    product = ordered(gather_fsdp(product, GEN), x, w).reshape(4, 4, 192, -1)
    product = swap_seq(jnp.roll(product, (-y, -z), (0, 1)), GEN)
    product = across(jnp.sum(product.astype(F32), axis=(0, 1)), GEN)
    product_high, product_low = split(product)
    term_crit = mm(product_high, head_in, 1, 1) + mm(product_low, head_in, 1, 1)

    back = direct4(across(direct4(after(input_grad, product), 1, CRIT), CRIT), 0, GEN)
    back = back.reshape(tokens, cols)
    term_gen = mm(gen_heads, back, 0, 0)

    stats = sent[:, :, HD:].astype(F32)
    margin = jnp.sum(stats[:, :, 18:21]) / tokens
    margin_back = across(jnp.broadcast_to(margin, (8, HD)), CRIT)[0, 0]
    margin = jnp.where(is_gen, margin_back, margin)
    signed = jnp.where(is_gen, margin, -margin)
    factor = jnp.where(is_gen, -1.0, 1.0) * jax.nn.sigmoid(signed)
    grads = (jnp.where(is_gen, term_gen, term_crit) * factor).astype(BF16)
    losses = jax.nn.softplus(signed).astype(BF16)
    return (grads[None], losses[None])


def solution(mesh):
    placed = (
        P("seq", None),
        P(None, None, "fsdp"),
        P(None, None, "fsdp"),
        P(),
        P(None, "seq", None),
        P("seq"),
        P("grp", None, "seq", "fsdp"),
        P("grp", "seq", "fsdp"),
        P("grp", None),
        P("fsdp", None),
        P(),
    )
    return jax.shard_map(
        local,
        mesh=mesh,
        in_specs=placed,
        out_specs=(P("grp", "seq", "fsdp"), P("grp")),
        check_vma=False,
    )
```

```python
import jax
import jax.numpy as jnp
from jax import lax
from jax.experimental import pallas as pl
from jax.experimental.pallas import tpu as pltpu
from jax.sharding import PartitionSpec as P

HD = 128
EPS = 1e-06
NEG = -1e30
AXES = ("grp", "seq", "fsdp")
VMEM = pltpu.CompilerParams(vmem_limit_bytes=50 * 2**20)
F32, BF16 = jnp.float32, jnp.bfloat16
GEN, CRIT = (0,), (1,)


def moved(value, step, groups=(0, 1), cross=False):
    dy, dz, dx, dw = step
    pairs = []
    for g in groups:
        for y in range(4):
            for z in range(4):
                for x in range(4):
                    for w in range(2):
                        there = 1 - g if cross else g
                        source = g * 128 + (4 * y + z) * 8 + 2 * x + w
                        target = (
                            there * 128
                            + (4 * ((y + dy) % 4) + (z + dz) % 4) * 8
                            + 2 * ((x + dx) % 4)
                            + (w + dw) % 2
                        )
                        pairs.append((source, target))
    return lax.ppermute(value, AXES, pairs)


def along(axis, k):
    step = [0, 0, 0, 0]
    step[axis] = k
    return tuple(step)


def direct4(value, axis, groups):
    return jnp.stack([value] + [moved(value, along(axis, k), groups) for k in (1, 2, 3)])


def gather_seq(lead, tail, groups):
    lead, tail = direct4(lead, 1, groups), direct4(tail, 0, groups)
    lead = direct4(lead, 0, groups)
    tail = jnp.stack([tail] + [moved(tail, along(1, k), groups) for k in (1, 2, 3)], axis=1)
    return [part.reshape((-1, part.shape[-1])) for part in (lead, tail)]


def spread(value, axis):
    count = lax.axis_size(axis)
    return lax.all_to_all(jnp.broadcast_to(value[None], (count,) + value.shape), axis, 0, 0)


def gather_out(shard, y, z):
    depth, width = shard.shape
    cut = 3 * HD

    def placed(value, axis, whole, at, new_axis):
        for k in range(4):
            piece = moved(value, along(axis, k), GEN) if k else value
            start = [0] * whole.ndim
            start[new_axis] = (at - k) % 4
            whole = lax.dynamic_update_slice(whole, jnp.expand_dims(piece, new_axis), start)
        return whole

    lead = placed(shard[:, :cut], 1, jnp.zeros((4, depth, cut), BF16), z, 0)
    tail = placed(shard[:, cut:], 0, jnp.zeros((4, depth, width - cut), BF16), y, 0)
    lead = placed(lead, 0, jnp.zeros((4, 4, depth, cut), BF16), y, 0)
    tail = placed(tail, 1, jnp.zeros((4, 4, depth, width - cut), BF16), z, 1)
    return [part.reshape(16 * depth, -1) for part in (lead, tail)]


def across(value, groups):
    return moved(value, (0, 0, 0, 0), groups, cross=True)


def after(value, other):
    first = other[(slice(0, 1),) * other.ndim].reshape(())
    return value + (first.astype(F32) * 0.0).astype(value.dtype)


def mm(a, b, ca, cb):
    return lax.dot_general(a, b, (((ca,), (cb,)), ((), ())), preferred_element_type=F32)


def generator_kernel(frames, mask, q, k0, k1, k2, v0, v1, v2, own_k, own_v, out):
    scale = HD ** (-0.5)
    query = q[...]
    parts = [mm(query, k[0], 1, 1) * scale for k in (k0, k1, k2)]
    own = mm(query, own_k[...], 1, 1) * scale
    parts.append(jnp.where(mask[0:1, :] > 0.5, own, NEG))
    top = parts[0].max(axis=-1, keepdims=True)
    for part in parts[1:]:
        top = jnp.maximum(top, part.max(axis=-1, keepdims=True))
    parts = [jnp.exp(part - top) for part in parts]
    total = sum(part.sum(axis=-1, keepdims=True) for part in parts)
    inverse = 1.0 / total
    values = [v0[0], v1[0], v2[0], own_v[...]]
    result = jnp.zeros(out.shape, F32)
    for part, value in zip(parts, values):
        result = result + mm((part * inverse).astype(BF16), value, 1, 0)
    out[...] = result.astype(BF16)


def generator_attention(frames, mask, query, cache_keys, cache_values, own_keys, own_values):
    rows, width = query.shape
    heads = width // HD
    count, length = own_keys.shape[0], cache_keys.shape[1]

    def picked(i):
        return pl.BlockSpec((1, length, HD), lambda h, f: (f[i], 0, h))

    return pl.pallas_call(
        generator_kernel,
        grid_spec=pltpu.PrefetchScalarGridSpec(
            num_scalar_prefetch=1,
            grid=(heads,),
            in_specs=[
                pl.BlockSpec(mask.shape, lambda h, f: (0, 0)),
                pl.BlockSpec((rows, HD), lambda h, f: (0, h)),
                picked(0),
                picked(1),
                picked(2),
                picked(0),
                picked(1),
                picked(2),
                pl.BlockSpec((count, HD), lambda h, f: (0, h)),
                pl.BlockSpec((count, HD), lambda h, f: (0, h)),
            ],
            out_specs=pl.BlockSpec((rows, HD), lambda h, f: (0, h)),
        ),
        out_shape=jax.ShapeDtypeStruct((rows, width), BF16),
        compiler_params=VMEM,
    )(
        frames, mask, query,
        cache_keys, cache_keys, cache_keys,
        cache_values, cache_values, cache_values,
        own_keys, own_values,
    )


def column(lead, tail, index):
    count = lead.shape[1] // HD
    ref, index = (lead, index) if index < count else (tail, index - count)
    return ref[:, index * HD : (index + 1) * HD]


def critic_kernel(q, lead, tail, out, lse):
    heads = q.shape[1] // HD
    for head in range(heads):
        here = slice(head * HD, (head + 1) * HD)
        scores = mm(q[:, here], column(lead, tail, head), 1, 1) * HD ** (-0.5)
        top = scores.max(axis=-1, keepdims=True)
        raised = jnp.exp(scores - top)
        total = raised.sum(axis=-1, keepdims=True)
        weights = (raised * (1.0 / total)).astype(BF16)
        out[:, here] = mm(weights, column(lead, tail, heads + head), 1, 0).astype(BF16)
        lse[:, here] = jnp.broadcast_to(top + jnp.log(total), (q.shape[0], HD))


def critic_attention(query, lead, tail):
    return pl.pallas_call(
        critic_kernel,
        out_shape=(
            jax.ShapeDtypeStruct(query.shape, BF16),
            jax.ShapeDtypeStruct(query.shape, F32),
        ),
        compiler_params=VMEM,
    )(query, lead, tail)


def query_kernel(q, lead, tail, lse, u, high, low, score, grad, sent):
    scale = HD ** (-0.5)
    width = q.shape[1]
    unit = u[...]
    stats = []
    for head, start in enumerate(range(0, width, HD)):
        here = slice(start, start + HD)
        keys = column(lead, tail, head)
        head_grad = (mm(unit, high[here, :], 1, 1) + mm(unit, low[here, :], 1, 1)).astype(BF16)
        logs = lse[:, start : start + 1]
        weights = jnp.exp(mm(q[:, here], keys, 1, 1) * scale - logs)
        slopes = mm(head_grad, column(lead, tail, width // HD + head), 1, 1)
        centred = jnp.sum(slopes * weights, axis=-1, keepdims=True)
        score_grad = (weights * (slopes - centred)).astype(BF16)
        grad[:, here] = (mm(score_grad, keys, 1, 0) * scale).astype(BF16)
        stats += [centred, logs]
    stats.append(score[...])
    lane = lax.broadcasted_iota(jnp.int32, (q.shape[0], HD), 1)
    table = jnp.zeros((q.shape[0], HD), F32)
    for i, stat in enumerate(stats):
        for j in range(3):
            term = stat.astype(BF16).astype(F32)
            table = jnp.where(lane == 3 * i + j, term, table)
            stat = stat - term
    sent[:, :HD] = unit
    sent[:, HD:] = table.astype(BF16)


def query_grads(query, lead, tail, lse, unit, high, low, score):
    rows, width = query.shape
    return pl.pallas_call(
        query_kernel,
        out_shape=(
            jax.ShapeDtypeStruct((rows, width), BF16),
            jax.ShapeDtypeStruct((rows, 2 * HD), BF16),
        ),
        compiler_params=VMEM,
    )(query, lead, tail, lse, unit, high, low, score)


def key_kernel(at, k, v, tail, sent, high, low, key_grad, value_grad, ordered_sent):
    scale = HD ** (-0.5)
    rows, width = k.shape
    y, z = at[0] // 4, at[0] % 4
    for dy in range(4):
        for dz in range(4):
            place = ((y + 4 - dy) % 4) * 4 + (z + 4 - dz) % 4
            block = (4 * dy + dz) * rows
            ordered_sent[block : block + rows, :] = sent[pl.ds(place, 1)][0]
    unit = ordered_sent[:, :HD]
    table = ordered_sent[:, HD:].astype(F32)

    def stat(i):
        return table[:, 3 * i : 3 * i + 1] + table[:, 3 * i + 1 : 3 * i + 2] + table[:, 3 * i + 2 : 3 * i + 3]

    first = tail.shape[1] - width
    for head, start in enumerate(range(0, width, HD)):
        here = slice(start, start + HD)
        queries = tail[:, first + start : first + start + HD]
        head_grad = (mm(unit, high[here, :], 1, 1) + mm(unit, low[here, :], 1, 1)).astype(BF16)
        weights = jnp.exp(mm(queries, k[:, here], 1, 1) * scale - stat(2 * head + 1))
        slopes = mm(head_grad, v[:, here], 1, 1)
        score_grad = (weights * (slopes - stat(2 * head))).astype(BF16)
        key_grad[:, here] = (mm(score_grad, queries, 0, 0) * scale).astype(BF16)
        value_grad[:, here] = mm(weights.astype(BF16), head_grad, 0, 0).astype(BF16)


def key_grads(at, keys, values, tail, sent, high, low):
    shape = jax.ShapeDtypeStruct(keys.shape, BF16)
    whole = pl.BlockSpec(memory_space=pltpu.VMEM)
    return pl.pallas_call(
        key_kernel,
        in_specs=[pl.BlockSpec(memory_space=pltpu.SMEM)] + [whole] * 6,
        out_shape=(shape, shape),
        scratch_shapes=[pltpu.VMEM((tail.shape[0], sent.shape[-1]), BF16)],
        compiler_params=VMEM,
    )(at, keys, values, tail, sent, high, low)


def product_kernel(at, heads, back, out, ordered_heads):
    rows = heads.shape[1]
    y, z = at[0] // 4, at[0] % 4
    for dy in range(4):
        for dz in range(4):
            place = ((y + 4 - dy) % 4) * 4 + (z + 4 - dz) % 4
            block = (4 * dy + dz) * rows
            ordered_heads[block : block + rows, :] = heads[pl.ds(place, 1)][0]
    out[...] = mm(ordered_heads[...], back[...], 0, 0)


def summed_product(at, heads, back):
    width = heads.shape[2]
    whole = pl.BlockSpec(memory_space=pltpu.VMEM)
    return pl.pallas_call(
        product_kernel,
        in_specs=[pl.BlockSpec(memory_space=pltpu.SMEM), whole, whole],
        out_shape=jax.ShapeDtypeStruct((width, back.shape[1]), F32),
        scratch_shapes=[pltpu.VMEM((back.shape[0], width), BF16)],
        compiler_params=VMEM,
    )(at, heads, back)


def split(value):
    high = lax.reduce_precision(value, 8, 7)
    return high.astype(BF16), (value - high).astype(BF16)


def normalised(row_block, gain_vector):
    lifted = row_block.astype(F32)
    inverse = lax.rsqrt(jnp.mean(lifted * lifted, axis=-1, keepdims=True) + EPS)
    return (lifted * inverse * gain_vector).astype(BF16), inverse


def times(a, b):
    return jnp.dot(a, b, preferred_element_type=F32).astype(BF16)


def unit_terms(units, head_out):
    active, back = jax.vjp(jax.nn.gelu, units)
    score = jnp.sum(active * head_out, axis=-1, keepdims=True)
    return score, back(jnp.broadcast_to(head_out, units.shape))[0].astype(BF16)


def pick_rows(real_bank, real_pick):
    chosen = jnp.zeros(real_bank.shape[1:], real_bank.dtype)
    for entry in range(real_bank.shape[0]):
        chosen = jnp.where((real_pick == entry)[:, None], real_bank[entry], chosen)
    return chosen


def local(
    new_rows, cache_keys, cache_values, cache_frames, real_bank, real_pick,
    attn_weights, out_weights, norm_gains, head_in, head_out,
):
    is_gen = lax.axis_index("grp") == 0
    seq_at, fsdp_at = lax.axis_index("seq"), lax.axis_index("fsdp")
    y, z, x, w = seq_at // 4, seq_at % 4, fsdp_at // 2, fsdp_at % 2
    rows, model = new_rows.shape
    cols = out_weights.shape[2]
    width = attn_weights.shape[3]
    tokens = rows * 16
    gains = norm_gains[0]
    start = fsdp_at * cols

    shard = jnp.concatenate([attn_weights[0, c] for c in range(3)], axis=1)
    weights = lax.all_gather(shard, "seq", axis=0, tiled=True)
    out_lead, out_tail = gather_out(out_weights[0], y, z)

    joint = jnp.dot(out_weights[0], head_in, preferred_element_type=F32)
    joint = spread(jnp.sum(spread(joint, "fsdp"), axis=0), "seq").reshape(8 * width, -1)
    high, low = split(lax.dynamic_slice_in_dim(joint, fsdp_at * width, width, 0))

    real_rows = pick_rows(real_bank, real_pick)
    first_rows = jnp.where(is_gen, new_rows, real_rows)
    first_normed, _ = normalised(first_rows, gains)
    first_normed = after(after(after(first_normed, high), out_lead), out_tail)
    first = times(first_normed, weights)
    first_q = first[:, :width]
    first_k, first_v = gather_seq(first[:, width : 2 * width], first[:, 2 * width :], (0, 1))
    key_y = (y - jnp.arange(tokens) // (4 * rows)) % 4
    mask = jnp.broadcast_to((key_y // 2 <= y // 2).astype(F32)[None], (8, tokens))
    first_heads = lax.cond(
        is_gen,
        lambda a: generator_attention(*a),
        lambda a: critic_attention(a[2], a[5], a[6])[0],
        (cache_frames, mask, first_q, cache_keys, cache_values, first_k, first_v),
    )

    first_all = spread(first_heads, "fsdp").transpose(1, 0, 2).reshape(rows, 8 * width)
    first_cols = lax.dynamic_slice_in_dim(first_rows, start, cols, 1).astype(F32)
    projected = [
        jnp.dot(first_all, part, preferred_element_type=F32) for part in (out_lead, out_tail)
    ]
    generated = (first_cols + jnp.concatenate(projected, axis=1)).astype(BF16)
    crossed = spread(across(generated, GEN), "fsdp")
    second_rows = crossed.transpose(1, 0, 2).reshape(rows, model)

    to_seq = after(first_all, generated).reshape(rows, 16, 192).transpose(1, 0, 2)
    gen_heads = lax.all_to_all(to_seq, "seq", 0, 0)

    def units_of(row_cols, heads):
        part = jnp.dot(row_cols, head_in, preferred_element_type=F32)
        part = part + jnp.dot(heads, high, preferred_element_type=F32)
        return part + jnp.dot(heads, low, preferred_element_type=F32)

    real_cols = lax.dynamic_slice_in_dim(first_rows, start, cols, 1)

    second_normed, inverse = normalised(second_rows, gains)
    second = times(second_normed, weights)
    second_q, second_k, second_v = (second[:, c * width : (c + 1) * width] for c in range(3))
    cut = width - HD
    every_lead, every_tail = gather_seq(
        jnp.concatenate([second_k, second_v[:, :cut]], axis=1),
        jnp.concatenate([second_v[:, cut:], second_q], axis=1),
        CRIT,
    )
    second_heads, lse = critic_attention(after(second_q, gen_heads), every_lead, every_tail)
    second_cols = lax.dynamic_slice_in_dim(second_rows, start, cols, 1)
    units = jnp.stack([units_of(real_cols, first_heads), units_of(second_cols, second_heads)])
    units = jnp.sum(spread(units, "fsdp"), axis=0)
    real_score, real_unit = unit_terms(units[0], head_out)
    fake_score, fake_unit = unit_terms(units[1], head_out)
    query_grad, sent = query_grads(
        second_q, every_lead, every_tail, lse, fake_unit, high, low, real_score - fake_score
    )
    sent = spread(sent, "seq")
    at = jnp.reshape(seq_at, (1,)).astype(jnp.int32)
    key_grad, value_grad = key_grads(at, second_k, second_v, every_tail, sent, high, low)
    grads = jnp.concatenate([query_grad, key_grad, value_grad], axis=1)
    row_terms = jnp.einsum(
        "tk,bnk->btn", grads, weights.reshape(8, cols, 3 * width), preferred_element_type=F32
    )
    row_terms = lax.all_to_all(row_terms.astype(BF16), "fsdp", 0, 0)
    row_grad = jnp.sum(row_terms.astype(F32), axis=0)
    gain_cols = lax.dynamic_slice_in_dim(gains, start, cols, 0)
    direction = mm(fake_unit, head_in, 1, 1)
    input_grad = (inverse * row_grad * gain_cols + direction).astype(BF16)

    product = mm(second_heads, fake_unit, 0, 0) - mm(first_heads, real_unit, 0, 0)
    product = spread(product.astype(BF16), "fsdp").reshape(16, 192, -1)
    product = lax.all_to_all(product, "seq", 0, 0)
    product_high, product_low = split(jnp.sum(product.astype(F32), axis=0))
    term_crit = mm(product_high, head_in, 1, 1) + mm(product_low, head_in, 1, 1)

    back = direct4(across(direct4(input_grad, 1, CRIT), CRIT), 0, GEN)
    back = back.reshape(tokens, cols)
    term_gen = summed_product(at, gen_heads, back)

    stats = sent[:, :, HD:].astype(F32)
    margin = jnp.sum(stats[:, :, 18:21]) / tokens
    margin_back = across(jnp.broadcast_to(margin, (8, HD)), CRIT)[0, 0]
    margin = jnp.where(is_gen, margin_back, margin)
    signed = jnp.where(is_gen, margin, -margin)
    factor = jnp.where(is_gen, -1.0, 1.0) * jax.nn.sigmoid(signed)
    grads = (jnp.where(is_gen, term_gen, term_crit) * factor).astype(BF16)
    losses = jax.nn.softplus(signed).astype(BF16)
    return (grads[None], losses[None])


def solution(mesh):
    placed = (
        P("seq", None),
        P(None, None, "fsdp"),
        P(None, None, "fsdp"),
        P(),
        P(None, "seq", None),
        P("seq"),
        P("grp", None, "seq", "fsdp"),
        P("grp", "seq", "fsdp"),
        P("grp", None),
        P("fsdp", None),
        P(),
    )
    return jax.shard_map(
        local,
        mesh=mesh,
        in_specs=placed,
        out_specs=(P("grp", "seq", "fsdp"), P("grp")),
        check_vma=False,
    )
```

```python
import jax
import jax.numpy as jnp
from jax import lax
from jax.experimental import pallas as pl
from jax.experimental.pallas import tpu as pltpu
from jax.sharding import PartitionSpec as P

HD = 128
EPS = 1e-06
NEG = -1e30
AXES = ("grp", "seq", "fsdp")
VMEM = pltpu.CompilerParams(vmem_limit_bytes=50 * 2**20)
F32, BF16 = jnp.float32, jnp.bfloat16


def moved(value, step, groups=(0, 1), cross=False):
    dy, dz, dx, dw = step
    pairs = []
    for g in groups:
        for y in range(4):
            for z in range(4):
                for x in range(4):
                    for w in range(2):
                        there = 1 - g if cross else g
                        source = g * 128 + (4 * y + z) * 8 + 2 * x + w
                        target = (
                            there * 128
                            + (4 * ((y + dy) % 4) + (z + dz) % 4) * 8
                            + 2 * ((x + dx) % 4)
                            + (w + dw) % 2
                        )
                        pairs.append((source, target))
    return lax.ppermute(value, AXES, pairs)


def along(axis, k):
    step = [0, 0, 0, 0]
    step[axis] = k
    return tuple(step)


def ring4(value, axis, groups):
    one = moved(value, along(axis, 1), groups)
    three = moved(value, along(axis, -1), groups)
    cut = value.ndim - 2
    half = value.shape[cut] // 2
    low = lax.slice_in_dim(one, 0, half, axis=cut)
    high = lax.slice_in_dim(three, half, 2 * half, axis=cut)
    low = moved(low, along(axis, 1), groups)
    high = moved(high, along(axis, -1), groups)
    return jnp.stack([value, one, jnp.concatenate([low, high], axis=cut), three])


def direct4(value, axis, groups):
    return jnp.stack([value] + [moved(value, along(axis, k), groups) for k in (1, 2, 3)])


def gather_seq(lead, tail, groups):
    lead, tail = direct4(lead, 1, groups), direct4(tail, 0, groups)
    lead = direct4(lead, 0, groups)
    tail = jnp.stack([tail] + [moved(tail, along(1, k), groups) for k in (1, 2, 3)], axis=1)
    return [part.reshape((-1, part.shape[-1])) for part in (lead, tail)]


def spread(value, axis):
    count = lax.axis_size(axis)
    return lax.all_to_all(jnp.broadcast_to(value[None], (count,) + value.shape), axis, 0, 0)


def across(value, groups):
    return moved(value, (0, 0, 0, 0), groups, cross=True)


def after(value, other):
    first = other[(slice(0, 1),) * other.ndim].reshape(())
    return value + (first.astype(F32) * 0.0).astype(value.dtype)


def mm(a, b, ca, cb):
    return lax.dot_general(a, b, (((ca,), (cb,)), ((), ())), preferred_element_type=F32)


def generator_kernel(frames, mask, q, k0, k1, k2, v0, v1, v2, own_k, own_v, out):
    scale = HD ** (-0.5)
    query = q[...]
    parts = [mm(query, k[0], 1, 1) * scale for k in (k0, k1, k2)]
    own = mm(query, own_k[...], 1, 1) * scale
    parts.append(jnp.where(mask[0:1, :] > 0.5, own, NEG))
    top = parts[0].max(axis=-1, keepdims=True)
    for part in parts[1:]:
        top = jnp.maximum(top, part.max(axis=-1, keepdims=True))
    parts = [jnp.exp(part - top) for part in parts]
    total = sum(part.sum(axis=-1, keepdims=True) for part in parts)
    inverse = 1.0 / total
    values = [v0[0], v1[0], v2[0], own_v[...]]
    result = jnp.zeros(out.shape, F32)
    for part, value in zip(parts, values):
        result = result + mm((part * inverse).astype(BF16), value, 1, 0)
    out[...] = result.astype(BF16)


def generator_attention(frames, mask, query, cache_keys, cache_values, key_value):
    rows, width = query.shape
    heads = width // HD
    count, length = key_value.shape[0], cache_keys.shape[1]

    def picked(i):
        return pl.BlockSpec((1, length, HD), lambda h, f: (f[i], 0, h))

    return pl.pallas_call(
        generator_kernel,
        grid_spec=pltpu.PrefetchScalarGridSpec(
            num_scalar_prefetch=1,
            grid=(heads,),
            in_specs=[
                pl.BlockSpec(mask.shape, lambda h, f: (0, 0)),
                pl.BlockSpec((rows, HD), lambda h, f: (0, h)),
                picked(0),
                picked(1),
                picked(2),
                picked(0),
                picked(1),
                picked(2),
                pl.BlockSpec((count, HD), lambda h, f: (0, h)),
                pl.BlockSpec((count, HD), lambda h, f: (0, heads + h)),
            ],
            out_specs=pl.BlockSpec((rows, HD), lambda h, f: (0, h)),
        ),
        out_shape=jax.ShapeDtypeStruct((rows, width), BF16),
        compiler_params=VMEM,
    )(
        frames, mask, query,
        cache_keys, cache_keys, cache_keys,
        cache_values, cache_values, cache_values,
        key_value, key_value,
    )


def column(lead, tail, index):
    count = lead.shape[1] // HD
    ref, index = (lead, index) if index < count else (tail, index - count)
    return ref[:, index * HD : (index + 1) * HD]


def critic_kernel(q, lead, tail, out, lse):
    heads = q.shape[1] // HD
    for head in range(heads):
        here = slice(head * HD, (head + 1) * HD)
        scores = mm(q[:, here], column(lead, tail, head), 1, 1) * HD ** (-0.5)
        top = scores.max(axis=-1, keepdims=True)
        raised = jnp.exp(scores - top)
        total = raised.sum(axis=-1, keepdims=True)
        weights = (raised * (1.0 / total)).astype(BF16)
        out[:, here] = mm(weights, column(lead, tail, heads + head), 1, 0).astype(BF16)
        lse[:, here] = jnp.broadcast_to(top + jnp.log(total), (q.shape[0], HD))


def critic_attention(query, lead, tail):
    return pl.pallas_call(
        critic_kernel,
        out_shape=(
            jax.ShapeDtypeStruct(query.shape, BF16),
            jax.ShapeDtypeStruct(query.shape, F32),
        ),
        compiler_params=VMEM,
    )(query, lead, tail)


def query_kernel(q, lead, tail, lse, u, high, low, score, grad, sent):
    scale = HD ** (-0.5)
    width = q.shape[1]
    unit = u[...]
    stats = []
    for head, start in enumerate(range(0, width, HD)):
        here = slice(start, start + HD)
        keys = column(lead, tail, head)
        head_grad = (mm(unit, high[here, :], 1, 1) + mm(unit, low[here, :], 1, 1)).astype(BF16)
        logs = lse[:, start : start + 1]
        weights = jnp.exp(mm(q[:, here], keys, 1, 1) * scale - logs)
        slopes = mm(head_grad, column(lead, tail, width // HD + head), 1, 1)
        centred = jnp.sum(slopes * weights, axis=-1, keepdims=True)
        score_grad = (weights * (slopes - centred)).astype(BF16)
        grad[:, here] = (mm(score_grad, keys, 1, 0) * scale).astype(BF16)
        stats += [centred, logs]
    stats.append(score[...])
    lane = lax.broadcasted_iota(jnp.int32, (q.shape[0], HD), 1)
    table = jnp.zeros((q.shape[0], HD), F32)
    for i, stat in enumerate(stats):
        for j in range(3):
            term = stat.astype(BF16).astype(F32)
            table = jnp.where(lane == 3 * i + j, term, table)
            stat = stat - term
    sent[:, :HD] = unit
    sent[:, HD:] = table.astype(BF16)


def query_grads(query, lead, tail, lse, unit, high, low, score):
    rows, width = query.shape
    return pl.pallas_call(
        query_kernel,
        out_shape=(
            jax.ShapeDtypeStruct((rows, width), BF16),
            jax.ShapeDtypeStruct((rows, 2 * HD), BF16),
        ),
        compiler_params=VMEM,
    )(query, lead, tail, lse, unit, high, low, score)


def key_kernel(at, k, v, tail, sent, high, low, key_grad, value_grad, ordered_sent):
    scale = HD ** (-0.5)
    rows, width = k.shape
    y, z = at[0] // 4, at[0] % 4
    for dy in range(4):
        for dz in range(4):
            place = ((y + 4 - dy) % 4) * 4 + (z + 4 - dz) % 4
            block = (4 * dy + dz) * rows
            ordered_sent[block : block + rows, :] = sent[pl.ds(place, 1)][0]
    unit = ordered_sent[:, :HD]
    table = ordered_sent[:, HD:].astype(F32)

    def stat(i):
        return table[:, 3 * i : 3 * i + 1] + table[:, 3 * i + 1 : 3 * i + 2] + table[:, 3 * i + 2 : 3 * i + 3]

    first = tail.shape[1] - width
    for head, start in enumerate(range(0, width, HD)):
        here = slice(start, start + HD)
        queries = tail[:, first + start : first + start + HD]
        head_grad = (mm(unit, high[here, :], 1, 1) + mm(unit, low[here, :], 1, 1)).astype(BF16)
        weights = jnp.exp(mm(queries, k[:, here], 1, 1) * scale - stat(2 * head + 1))
        slopes = mm(head_grad, v[:, here], 1, 1)
        score_grad = (weights * (slopes - stat(2 * head))).astype(BF16)
        key_grad[:, here] = (mm(score_grad, queries, 0, 0) * scale).astype(BF16)
        value_grad[:, here] = mm(weights.astype(BF16), head_grad, 0, 0).astype(BF16)


def key_grads(at, keys, values, tail, sent, high, low):
    shape = jax.ShapeDtypeStruct(keys.shape, BF16)
    whole = pl.BlockSpec(memory_space=pltpu.VMEM)
    return pl.pallas_call(
        key_kernel,
        in_specs=[pl.BlockSpec(memory_space=pltpu.SMEM)] + [whole] * 6,
        out_shape=(shape, shape),
        scratch_shapes=[pltpu.VMEM((tail.shape[0], sent.shape[-1]), BF16)],
        compiler_params=VMEM,
    )(at, keys, values, tail, sent, high, low)


def product_kernel(at, heads, back, out, ordered_heads):
    rows = heads.shape[1]
    y, z = at[0] // 4, at[0] % 4
    for dy in range(4):
        for dz in range(4):
            place = ((y + 4 - dy) % 4) * 4 + (z + 4 - dz) % 4
            block = (4 * dy + dz) * rows
            ordered_heads[block : block + rows, :] = heads[pl.ds(place, 1)][0]
    out[...] = mm(ordered_heads[...], back[...], 0, 0)


def summed_product(at, heads, back):
    width = heads.shape[2]
    whole = pl.BlockSpec(memory_space=pltpu.VMEM)
    return pl.pallas_call(
        product_kernel,
        in_specs=[pl.BlockSpec(memory_space=pltpu.SMEM), whole, whole],
        out_shape=jax.ShapeDtypeStruct((width, back.shape[1]), F32),
        scratch_shapes=[pltpu.VMEM((back.shape[0], width), BF16)],
        compiler_params=VMEM,
    )(at, heads, back)


def split(value):
    high = lax.reduce_precision(value, 8, 7)
    return high.astype(BF16), (value - high).astype(BF16)


def normalised(row_block, gain_vector):
    lifted = row_block.astype(F32)
    inverse = lax.rsqrt(jnp.mean(lifted * lifted, axis=-1, keepdims=True) + EPS)
    return (lifted * inverse * gain_vector).astype(BF16), inverse


def times(a, b):
    return jnp.dot(a, b, preferred_element_type=F32).astype(BF16)


def unit_terms(units, head_out):
    active, back = jax.vjp(jax.nn.gelu, units)
    score = jnp.sum(active * head_out, axis=-1, keepdims=True)
    return score, back(jnp.broadcast_to(head_out, units.shape))[0].astype(BF16)


def pick_rows(real_bank, real_pick):
    chosen = jnp.zeros(real_bank.shape[1:], real_bank.dtype)
    for entry in range(real_bank.shape[0]):
        chosen = jnp.where((real_pick == entry)[:, None], real_bank[entry], chosen)
    return chosen


GEN, CRIT = (0,), (1,)


def local(
    new_rows, cache_keys, cache_values, cache_frames, real_bank, real_pick,
    attn_weights, out_weights, norm_gains, head_in, head_out,
):
    is_gen = lax.axis_index("grp") == 0
    seq_at, fsdp_at = lax.axis_index("seq"), lax.axis_index("fsdp")
    y, z, x, w = seq_at // 4, seq_at % 4, fsdp_at // 2, fsdp_at % 2
    rows, model = new_rows.shape
    cols = out_weights.shape[2]
    width = attn_weights.shape[3]
    tokens = rows * 16
    gains = norm_gains[0]
    start = fsdp_at * cols

    shard = jnp.concatenate([attn_weights[0, c] for c in range(3)], axis=1)
    weights = lax.all_gather(shard, "seq", axis=0, tiled=True)
    full_out = lax.all_gather(out_weights[0], "seq", axis=0, tiled=True)

    real_rows = pick_rows(real_bank, real_pick)
    first_rows = jnp.where(is_gen, new_rows, real_rows)
    first_normed, _ = normalised(first_rows, gains)
    first = times(first_normed, weights)
    first_q = first[:, :width]
    first_kv = ring4(ring4(first[:, width:], 1, (0, 1)), 0, (0, 1)).reshape(tokens, 2 * width)
    key_y = (y - jnp.arange(tokens) // (4 * rows)) % 4
    mask = jnp.broadcast_to((key_y // 2 <= y // 2).astype(F32)[None], (8, tokens))
    first_heads = lax.cond(
        is_gen,
        lambda a: generator_attention(*a),
        lambda a: critic_attention(a[2], a[5], a[2])[0],
        (cache_frames, mask, first_q, cache_keys, cache_values, first_kv),
    )

    first_all = spread(first_heads, "fsdp").transpose(1, 0, 2).reshape(rows, 8 * width)
    first_cols = lax.dynamic_slice_in_dim(first_rows, start, cols, 1).astype(F32)
    generated = (first_cols + jnp.dot(first_all, full_out, preferred_element_type=F32)).astype(BF16)
    crossed = spread(across(generated, GEN), "fsdp")
    second_rows = crossed.transpose(1, 0, 2).reshape(rows, model)

    to_seq = after(first_all, crossed).reshape(rows, 16, 192).transpose(1, 0, 2)
    gen_heads = lax.all_to_all(to_seq, "seq", 0, 0)

    joint = jnp.dot(full_out, head_in, preferred_element_type=F32)
    high, low = split(lax.psum_scatter(joint, "fsdp", scatter_dimension=0, tiled=True))

    def units_of(row_cols, heads):
        part = jnp.dot(row_cols, head_in, preferred_element_type=F32)
        part = part + jnp.dot(heads, high, preferred_element_type=F32)
        return part + jnp.dot(heads, low, preferred_element_type=F32)

    real_cols = lax.dynamic_slice_in_dim(first_rows, start, cols, 1)

    second_normed, inverse = normalised(second_rows, gains)
    second = times(second_normed, weights)
    second_q, second_k, second_v = (second[:, c * width : (c + 1) * width] for c in range(3))
    cut = width - HD
    every_lead, every_tail = gather_seq(
        jnp.concatenate([second_k, second_v[:, :cut]], axis=1),
        jnp.concatenate([second_v[:, cut:], second_q], axis=1),
        CRIT,
    )
    second_heads, lse = critic_attention(after(second_q, gen_heads), every_lead, every_tail)
    second_cols = lax.dynamic_slice_in_dim(second_rows, start, cols, 1)
    units = jnp.stack([units_of(real_cols, after(first_heads, second_heads)), units_of(second_cols, second_heads)])
    units = jnp.sum(spread(units, "fsdp"), axis=0)
    real_score, real_unit = unit_terms(units[0], head_out)
    fake_score, fake_unit = unit_terms(units[1], head_out)
    query_grad, sent = query_grads(
        second_q, every_lead, every_tail, lse, fake_unit, high, low, real_score - fake_score
    )
    sent = spread(sent, "seq")
    at = jnp.reshape(seq_at, (1,)).astype(jnp.int32)
    key_grad, value_grad = key_grads(at, second_k, second_v, every_tail, sent, high, low)
    grads = jnp.concatenate([query_grad, key_grad, value_grad], axis=1)
    row_terms = jnp.einsum(
        "tk,bnk->btn", grads, weights.reshape(8, cols, 3 * width), preferred_element_type=F32
    )
    row_terms = lax.all_to_all(row_terms.astype(BF16), "fsdp", 0, 0)
    row_grad = jnp.sum(row_terms.astype(F32), axis=0)
    gain_cols = lax.dynamic_slice_in_dim(gains, start, cols, 0)
    direction = mm(fake_unit, head_in, 1, 1)
    input_grad = (inverse * row_grad * gain_cols + direction).astype(BF16)

    product = mm(second_heads, fake_unit, 0, 0) - mm(first_heads, real_unit, 0, 0)
    product = spread(product.astype(BF16), "fsdp").reshape(16, 192, -1)
    product = lax.all_to_all(product, "seq", 0, 0)
    product_high, product_low = split(jnp.sum(product.astype(F32), axis=0))
    term_crit = mm(product_high, head_in, 1, 1) + mm(product_low, head_in, 1, 1)

    back = direct4(across(direct4(input_grad, 1, CRIT), CRIT), 0, GEN)
    back = back.reshape(tokens, cols)
    term_gen = summed_product(at, gen_heads, back)

    stats = sent[:, :, HD:].astype(F32)
    margin = jnp.sum(stats[:, :, 18:21]) / tokens
    margin_back = across(jnp.broadcast_to(margin, (8, HD)), CRIT)[0, 0]
    margin = jnp.where(is_gen, margin_back, margin)
    signed = jnp.where(is_gen, margin, -margin)
    factor = jnp.where(is_gen, -1.0, 1.0) * jax.nn.sigmoid(signed)
    grads = (jnp.where(is_gen, term_gen, term_crit) * factor).astype(BF16)
    losses = jax.nn.softplus(signed).astype(BF16)
    return (grads[None], losses[None])


def solution(mesh):
    placed = (
        P("seq", None),
        P(None, None, "fsdp"),
        P(None, None, "fsdp"),
        P(),
        P(None, "seq", None),
        P("seq"),
        P("grp", None, "seq", "fsdp"),
        P("grp", "seq", "fsdp"),
        P("grp", None),
        P("fsdp", None),
        P(),
    )
    return jax.shard_map(
        local,
        mesh=mesh,
        in_specs=placed,
        out_specs=(P("grp", "seq", "fsdp"), P("grp")),
        check_vma=False,
    )
```

```python
import jax
import jax.numpy as jnp
from jax import lax
from jax.experimental import pallas as pl
from jax.experimental.pallas import tpu as pltpu
from jax.sharding import PartitionSpec as P

HD = 128
EPS = 1e-06
NEG = -1e30
AXES = ("grp", "seq", "fsdp")
VMEM = pltpu.CompilerParams(vmem_limit_bytes=50 * 2**20)
F32, BF16 = jnp.float32, jnp.bfloat16


def moved(value, step, groups=(0, 1), cross=False):
    dy, dz, dx, dw = step
    pairs = []
    for g in groups:
        for y in range(4):
            for z in range(4):
                for x in range(4):
                    for w in range(2):
                        there = 1 - g if cross else g
                        source = g * 128 + (4 * y + z) * 8 + 2 * x + w
                        target = (
                            there * 128
                            + (4 * ((y + dy) % 4) + (z + dz) % 4) * 8
                            + 2 * ((x + dx) % 4)
                            + (w + dw) % 2
                        )
                        pairs.append((source, target))
    return lax.ppermute(value, AXES, pairs)


def along(axis, k):
    step = [0, 0, 0, 0]
    step[axis] = k
    return tuple(step)


def ring4(value, axis, groups):
    one = moved(value, along(axis, 1), groups)
    three = moved(value, along(axis, -1), groups)
    cut = value.ndim - 2
    half = value.shape[cut] // 2
    low = lax.slice_in_dim(one, 0, half, axis=cut)
    high = lax.slice_in_dim(three, half, 2 * half, axis=cut)
    low = moved(low, along(axis, 1), groups)
    high = moved(high, along(axis, -1), groups)
    return jnp.stack([value, one, jnp.concatenate([low, high], axis=cut), three])


def direct4(value, axis, groups):
    return jnp.stack([value] + [moved(value, along(axis, k), groups) for k in (1, 2, 3)])


def gather_seq(lead, tail, groups):
    lead, tail = direct4(lead, 1, groups), direct4(tail, 0, groups)
    lead = direct4(lead, 0, groups)
    tail = jnp.stack([tail] + [moved(tail, along(1, k), groups) for k in (1, 2, 3)], axis=1)
    return [part.reshape((-1, part.shape[-1])) for part in (lead, tail)]


def spread(value, axis):
    count = lax.axis_size(axis)
    return lax.all_to_all(jnp.broadcast_to(value[None], (count,) + value.shape), axis, 0, 0)


def swap_seq(blocks, groups):
    rows = [blocks[0]] + [moved(blocks[k], along(0, k), groups) for k in (1, 2, 3)]
    rows = jnp.stack(rows)
    cols = [rows[:, 0]] + [moved(rows[:, k], along(1, k), groups) for k in (1, 2, 3)]
    return jnp.stack(cols, axis=1)


def across(value, groups):
    return moved(value, (0, 0, 0, 0), groups, cross=True)


def after(value, other):
    first = other[(slice(0, 1),) * other.ndim].reshape(())
    return value + (first.astype(F32) * 0.0).astype(value.dtype)


def mm(a, b, ca, cb):
    return lax.dot_general(a, b, (((ca,), (cb,)), ((), ())), preferred_element_type=F32)


def generator_kernel(frames, mask, q, k0, k1, k2, v0, v1, v2, own_k, own_v, out):
    scale = HD ** (-0.5)
    query = q[...]
    parts = [mm(query, k[0], 1, 1) * scale for k in (k0, k1, k2)]
    own = mm(query, own_k[...], 1, 1) * scale
    parts.append(jnp.where(mask[0:1, :] > 0.5, own, NEG))
    top = parts[0].max(axis=-1, keepdims=True)
    for part in parts[1:]:
        top = jnp.maximum(top, part.max(axis=-1, keepdims=True))
    parts = [jnp.exp(part - top) for part in parts]
    total = sum(part.sum(axis=-1, keepdims=True) for part in parts)
    inverse = 1.0 / total
    values = [v0[0], v1[0], v2[0], own_v[...]]
    result = jnp.zeros(out.shape, F32)
    for part, value in zip(parts, values):
        result = result + mm((part * inverse).astype(BF16), value, 1, 0)
    out[...] = result.astype(BF16)


def generator_attention(frames, mask, query, cache_keys, cache_values, own_keys, own_values):
    rows, width = query.shape
    heads = width // HD
    count, length = own_keys.shape[0], cache_keys.shape[1]

    def picked(i):
        return pl.BlockSpec((1, length, HD), lambda h, f: (f[i], 0, h))

    return pl.pallas_call(
        generator_kernel,
        grid_spec=pltpu.PrefetchScalarGridSpec(
            num_scalar_prefetch=1,
            grid=(heads,),
            in_specs=[
                pl.BlockSpec(mask.shape, lambda h, f: (0, 0)),
                pl.BlockSpec((rows, HD), lambda h, f: (0, h)),
                picked(0),
                picked(1),
                picked(2),
                picked(0),
                picked(1),
                picked(2),
                pl.BlockSpec((count, HD), lambda h, f: (0, h)),
                pl.BlockSpec((count, HD), lambda h, f: (0, h)),
            ],
            out_specs=pl.BlockSpec((rows, HD), lambda h, f: (0, h)),
        ),
        out_shape=jax.ShapeDtypeStruct((rows, width), BF16),
        compiler_params=VMEM,
    )(
        frames, mask, query,
        cache_keys, cache_keys, cache_keys,
        cache_values, cache_values, cache_values,
        own_keys, own_values,
    )


def column(lead, tail, index):
    count = lead.shape[1] // HD
    ref, index = (lead, index) if index < count else (tail, index - count)
    return ref[:, index * HD : (index + 1) * HD]


def critic_kernel(q, lead, tail, out, lse):
    heads = q.shape[1] // HD
    for head in range(heads):
        here = slice(head * HD, (head + 1) * HD)
        scores = mm(q[:, here], column(lead, tail, head), 1, 1) * HD ** (-0.5)
        top = scores.max(axis=-1, keepdims=True)
        raised = jnp.exp(scores - top)
        total = raised.sum(axis=-1, keepdims=True)
        weights = (raised * (1.0 / total)).astype(BF16)
        out[:, here] = mm(weights, column(lead, tail, heads + head), 1, 0).astype(BF16)
        lse[:, here] = jnp.broadcast_to(top + jnp.log(total), (q.shape[0], HD))


def critic_attention(query, lead, tail):
    return pl.pallas_call(
        critic_kernel,
        out_shape=(
            jax.ShapeDtypeStruct(query.shape, BF16),
            jax.ShapeDtypeStruct(query.shape, F32),
        ),
        compiler_params=VMEM,
    )(query, lead, tail)


def query_kernel(q, lead, tail, lse, u, high, low, score, grad, sent):
    scale = HD ** (-0.5)
    width = q.shape[1]
    unit = u[...]
    stats = []
    for head, start in enumerate(range(0, width, HD)):
        here = slice(start, start + HD)
        keys = column(lead, tail, head)
        head_grad = (mm(unit, high[here, :], 1, 1) + mm(unit, low[here, :], 1, 1)).astype(BF16)
        logs = lse[:, start : start + 1]
        weights = jnp.exp(mm(q[:, here], keys, 1, 1) * scale - logs)
        slopes = mm(head_grad, column(lead, tail, width // HD + head), 1, 1)
        centred = jnp.sum(slopes * weights, axis=-1, keepdims=True)
        score_grad = (weights * (slopes - centred)).astype(BF16)
        grad[:, here] = (mm(score_grad, keys, 1, 0) * scale).astype(BF16)
        stats += [centred, logs]
    stats.append(score[...])
    lane = lax.broadcasted_iota(jnp.int32, (q.shape[0], HD), 1)
    table = jnp.zeros((q.shape[0], HD), F32)
    for i, stat in enumerate(stats):
        for j in range(3):
            term = stat.astype(BF16).astype(F32)
            table = jnp.where(lane == 3 * i + j, term, table)
            stat = stat - term
    sent[:, :HD] = unit
    sent[:, HD:] = table.astype(BF16)


def query_grads(query, lead, tail, lse, unit, high, low, score):
    rows, width = query.shape
    return pl.pallas_call(
        query_kernel,
        out_shape=(
            jax.ShapeDtypeStruct((rows, width), BF16),
            jax.ShapeDtypeStruct((rows, 2 * HD), BF16),
        ),
        compiler_params=VMEM,
    )(query, lead, tail, lse, unit, high, low, score)


def key_kernel(at, k, v, tail, sent, high, low, key_grad, value_grad, ordered_sent):
    scale = HD ** (-0.5)
    rows, width = k.shape
    y, z = at[0] // 4, at[0] % 4
    for dy in range(4):
        for dz in range(4):
            place = ((y + 4 - dy) % 4) * 4 + (z + 4 - dz) % 4
            block = (4 * dy + dz) * rows
            ordered_sent[block : block + rows, :] = sent[pl.ds(place, 1)][0]
    unit = ordered_sent[:, :HD]
    table = ordered_sent[:, HD:].astype(F32)

    def stat(i):
        return table[:, 3 * i : 3 * i + 1] + table[:, 3 * i + 1 : 3 * i + 2] + table[:, 3 * i + 2 : 3 * i + 3]

    first = tail.shape[1] - width
    for head, start in enumerate(range(0, width, HD)):
        here = slice(start, start + HD)
        queries = tail[:, first + start : first + start + HD]
        head_grad = (mm(unit, high[here, :], 1, 1) + mm(unit, low[here, :], 1, 1)).astype(BF16)
        weights = jnp.exp(mm(queries, k[:, here], 1, 1) * scale - stat(2 * head + 1))
        slopes = mm(head_grad, v[:, here], 1, 1)
        score_grad = (weights * (slopes - stat(2 * head))).astype(BF16)
        key_grad[:, here] = (mm(score_grad, queries, 0, 0) * scale).astype(BF16)
        value_grad[:, here] = mm(weights.astype(BF16), head_grad, 0, 0).astype(BF16)


def key_grads(at, keys, values, tail, sent, high, low):
    shape = jax.ShapeDtypeStruct(keys.shape, BF16)
    whole = pl.BlockSpec(memory_space=pltpu.VMEM)
    return pl.pallas_call(
        key_kernel,
        in_specs=[pl.BlockSpec(memory_space=pltpu.SMEM)] + [whole] * 6,
        out_shape=(shape, shape),
        scratch_shapes=[pltpu.VMEM((tail.shape[0], sent.shape[-1]), BF16)],
        compiler_params=VMEM,
    )(at, keys, values, tail, sent, high, low)


def split(value):
    high = lax.reduce_precision(value, 8, 7)
    return high.astype(BF16), (value - high).astype(BF16)


def normalised(row_block, gain_vector):
    lifted = row_block.astype(F32)
    inverse = lax.rsqrt(jnp.mean(lifted * lifted, axis=-1, keepdims=True) + EPS)
    return (lifted * inverse * gain_vector).astype(BF16), inverse


def times(a, b):
    return jnp.dot(a, b, preferred_element_type=F32).astype(BF16)


def unit_terms(units, head_out):
    active, back = jax.vjp(jax.nn.gelu, units)
    score = jnp.sum(active * head_out, axis=-1, keepdims=True)
    return score, back(jnp.broadcast_to(head_out, units.shape))[0].astype(BF16)


def pick_rows(real_bank, real_pick):
    chosen = jnp.zeros(real_bank.shape[1:], real_bank.dtype)
    for entry in range(real_bank.shape[0]):
        chosen = jnp.where((real_pick == entry)[:, None], real_bank[entry], chosen)
    return chosen


GEN, CRIT = (0,), (1,)


def local(
    new_rows, cache_keys, cache_values, cache_frames, real_bank, real_pick,
    attn_weights, out_weights, norm_gains, head_in, head_out,
):
    is_gen = lax.axis_index("grp") == 0
    seq_at, fsdp_at = lax.axis_index("seq"), lax.axis_index("fsdp")
    y, z, x, w = seq_at // 4, seq_at % 4, fsdp_at // 2, fsdp_at % 2
    rows, model = new_rows.shape
    cols = out_weights.shape[2]
    width = attn_weights.shape[3]
    tokens = rows * 16
    gains = norm_gains[0]
    start = fsdp_at * cols

    shard = jnp.concatenate([attn_weights[0, c] for c in range(3)], axis=1)
    weights = lax.all_gather(shard, "seq", axis=0, tiled=True)
    full_out = lax.all_gather(out_weights[0], "seq", axis=0, tiled=True)

    real_rows = pick_rows(real_bank, real_pick)
    first_rows = jnp.where(is_gen, new_rows, real_rows)
    first_normed, _ = normalised(first_rows, gains)
    first = times(first_normed, weights)
    first_q = first[:, :width]
    first_kv = ring4(ring4(first[:, width:], 1, (0, 1)), 0, (0, 1)).reshape(tokens, 2 * width)
    first_k, first_v = first_kv[:, :width], first_kv[:, width:]
    key_y = (y - jnp.arange(tokens) // (4 * rows)) % 4
    mask = jnp.broadcast_to((key_y // 2 <= y // 2).astype(F32)[None], (8, tokens))
    first_heads = lax.cond(
        is_gen,
        lambda a: generator_attention(*a),
        lambda a: critic_attention(a[2], a[5], a[6])[0],
        (cache_frames, mask, first_q, cache_keys, cache_values, first_k, first_v),
    )

    joint = jnp.dot(full_out, head_in, preferred_element_type=F32)
    first_all = spread(first_heads, "fsdp").transpose(1, 0, 2).reshape(rows, 8 * width)
    first_all = after(first_all, joint)
    first_cols = lax.dynamic_slice_in_dim(first_rows, start, cols, 1).astype(F32)
    generated = (first_cols + jnp.dot(first_all, full_out, preferred_element_type=F32)).astype(BF16)
    crossed = spread(across(generated, GEN), "fsdp")
    second_rows = crossed.transpose(1, 0, 2).reshape(rows, model)

    to_seq = first_all.reshape(rows, 4, 4, 192).transpose(1, 2, 0, 3)
    gen_heads = swap_seq(jnp.roll(to_seq, (-y, -z), (0, 1)), GEN).reshape(tokens, 192)

    high, low = split(lax.psum_scatter(joint, "fsdp", scatter_dimension=0, tiled=True))

    def units_of(row_cols, heads):
        part = jnp.dot(row_cols, head_in, preferred_element_type=F32)
        part = part + jnp.dot(heads, high, preferred_element_type=F32)
        return part + jnp.dot(heads, low, preferred_element_type=F32)

    real_cols = lax.dynamic_slice_in_dim(first_rows, start, cols, 1)

    second_normed, inverse = normalised(second_rows, gains)
    second = times(second_normed, weights)
    second_q, second_k, second_v = (second[:, c * width : (c + 1) * width] for c in range(3))
    cut = width - HD
    every_lead, every_tail = gather_seq(
        jnp.concatenate([second_k, second_v[:, :cut]], axis=1),
        jnp.concatenate([second_v[:, cut:], second_q], axis=1),
        CRIT,
    )
    second_heads, lse = critic_attention(second_q, every_lead, every_tail)
    second_cols = lax.dynamic_slice_in_dim(second_rows, start, cols, 1)
    units = jnp.stack([units_of(real_cols, after(first_heads, second_heads)), units_of(second_cols, second_heads)])
    units = after(jnp.sum(spread(units, "fsdp"), axis=0), gen_heads)
    real_score, real_unit = unit_terms(units[0], head_out)
    fake_score, fake_unit = unit_terms(units[1], head_out)
    query_grad, sent = query_grads(
        second_q, every_lead, every_tail, lse, fake_unit, high, low, real_score - fake_score
    )
    sent = spread(sent, "seq")
    at = jnp.reshape(seq_at, (1,)).astype(jnp.int32)
    key_grad, value_grad = key_grads(at, second_k, second_v, every_tail, sent, high, low)
    grads = jnp.concatenate([query_grad, key_grad, value_grad], axis=1)
    row_terms = jnp.einsum(
        "tk,bnk->btn", grads, weights.reshape(8, cols, 3 * width), preferred_element_type=F32
    )
    row_terms = lax.all_to_all(row_terms.astype(BF16), "fsdp", 0, 0)
    row_grad = jnp.sum(row_terms.astype(F32), axis=0)
    gain_cols = lax.dynamic_slice_in_dim(gains, start, cols, 0)
    direction = mm(fake_unit, head_in, 1, 1)
    input_grad = (inverse * row_grad * gain_cols + direction).astype(BF16)

    product = mm(second_heads, fake_unit, 0, 0) - mm(first_heads, real_unit, 0, 0)
    product = spread(product.astype(BF16), "fsdp").reshape(16, 192, -1)
    product = lax.all_to_all(product, "seq", 0, 0)
    product_high, product_low = split(jnp.sum(product.astype(F32), axis=0))
    term_crit = mm(product_high, head_in, 1, 1) + mm(product_low, head_in, 1, 1)

    back = direct4(across(direct4(input_grad, 1, CRIT), CRIT), 0, GEN)
    back = back.reshape(tokens, cols)
    term_gen = mm(gen_heads, back, 0, 0)

    stats = sent[:, :, HD:].astype(F32)
    margin = jnp.sum(stats[:, :, 18:21]) / tokens
    margin_back = across(jnp.broadcast_to(margin, (8, HD)), CRIT)[0, 0]
    margin = jnp.where(is_gen, margin_back, margin)
    signed = jnp.where(is_gen, margin, -margin)
    factor = jnp.where(is_gen, -1.0, 1.0) * jax.nn.sigmoid(signed)
    grads = (jnp.where(is_gen, term_gen, term_crit) * factor).astype(BF16)
    losses = jax.nn.softplus(signed).astype(BF16)
    return (grads[None], losses[None])


def solution(mesh):
    placed = (
        P("seq", None),
        P(None, None, "fsdp"),
        P(None, None, "fsdp"),
        P(),
        P(None, "seq", None),
        P("seq"),
        P("grp", None, "seq", "fsdp"),
        P("grp", "seq", "fsdp"),
        P("grp", None),
        P("fsdp", None),
        P(),
    )
    return jax.shard_map(
        local,
        mesh=mesh,
        in_specs=placed,
        out_specs=(P("grp", "seq", "fsdp"), P("grp")),
        check_vma=False,
    )
```

```python
import jax
import jax.numpy as jnp
from jax import lax
from jax.experimental import pallas as pl
from jax.experimental.pallas import tpu as pltpu
from jax.sharding import PartitionSpec as P

HD = 128
EPS = 1e-06
NEG = -1e30
AXES = ("grp", "seq", "fsdp")
VMEM = pltpu.CompilerParams(vmem_limit_bytes=50 * 2**20)
F32, BF16 = jnp.float32, jnp.bfloat16


def moved(value, step, groups=(0, 1), cross=False):
    dy, dz, dx, dw = step
    pairs = []
    for g in groups:
        for y in range(4):
            for z in range(4):
                for x in range(4):
                    for w in range(2):
                        there = 1 - g if cross else g
                        source = g * 128 + (4 * y + z) * 8 + 2 * x + w
                        target = (
                            there * 128
                            + (4 * ((y + dy) % 4) + (z + dz) % 4) * 8
                            + 2 * ((x + dx) % 4)
                            + (w + dw) % 2
                        )
                        pairs.append((source, target))
    return lax.ppermute(value, AXES, pairs)


def along(axis, k):
    step = [0, 0, 0, 0]
    step[axis] = k
    return tuple(step)


def ring4(value, axis, groups):
    one = moved(value, along(axis, 1), groups)
    three = moved(value, along(axis, -1), groups)
    cut = value.ndim - 2
    half = value.shape[cut] // 2
    low = lax.slice_in_dim(one, 0, half, axis=cut)
    high = lax.slice_in_dim(three, half, 2 * half, axis=cut)
    low = moved(low, along(axis, 1), groups)
    high = moved(high, along(axis, -1), groups)
    return jnp.stack([value, one, jnp.concatenate([low, high], axis=cut), three])


def direct4(value, axis, groups):
    return jnp.stack([value] + [moved(value, along(axis, k), groups) for k in (1, 2, 3)])


def gather_seq(lead, tail, groups):
    lead, tail = direct4(lead, 1, groups), direct4(tail, 0, groups)
    lead = direct4(lead, 0, groups)
    tail = jnp.stack([tail] + [moved(tail, along(1, k), groups) for k in (1, 2, 3)], axis=1)
    return [part.reshape((-1, part.shape[-1])) for part in (lead, tail)]


def spread(value, axis):
    count = lax.axis_size(axis)
    return lax.all_to_all(jnp.broadcast_to(value[None], (count,) + value.shape), axis, 0, 0)


def swap_seq(blocks, groups):
    rows = [blocks[0]] + [moved(blocks[k], along(0, k), groups) for k in (1, 2, 3)]
    rows = jnp.stack(rows)
    cols = [rows[:, 0]] + [moved(rows[:, k], along(1, k), groups) for k in (1, 2, 3)]
    return jnp.stack(cols, axis=1)


def across(value, groups):
    return moved(value, (0, 0, 0, 0), groups, cross=True)


def after(value, other):
    first = other[(slice(0, 1),) * other.ndim].reshape(())
    return value + (first.astype(F32) * 0.0).astype(value.dtype)


def mm(a, b, ca, cb):
    return lax.dot_general(a, b, (((ca,), (cb,)), ((), ())), preferred_element_type=F32)


def generator_kernel(frames, mask, q, k0, k1, k2, v0, v1, v2, own_k, own_v, out):
    scale = HD ** (-0.5)
    query = q[...]
    parts = [mm(query, k[0], 1, 1) * scale for k in (k0, k1, k2)]
    own = mm(query, own_k[...], 1, 1) * scale
    parts.append(jnp.where(mask[0:1, :] > 0.5, own, NEG))
    top = parts[0].max(axis=-1, keepdims=True)
    for part in parts[1:]:
        top = jnp.maximum(top, part.max(axis=-1, keepdims=True))
    parts = [jnp.exp(part - top) for part in parts]
    total = sum(part.sum(axis=-1, keepdims=True) for part in parts)
    inverse = 1.0 / total
    values = [v0[0], v1[0], v2[0], own_v[...]]
    result = jnp.zeros(out.shape, F32)
    for part, value in zip(parts, values):
        result = result + mm((part * inverse).astype(BF16), value, 1, 0)
    out[...] = result.astype(BF16)


def generator_attention(frames, mask, query, cache_keys, cache_values, own_keys, own_values):
    rows, width = query.shape
    heads = width // HD
    count, length = own_keys.shape[0], cache_keys.shape[1]

    def picked(i):
        return pl.BlockSpec((1, length, HD), lambda h, f: (f[i], 0, h))

    return pl.pallas_call(
        generator_kernel,
        grid_spec=pltpu.PrefetchScalarGridSpec(
            num_scalar_prefetch=1,
            grid=(heads,),
            in_specs=[
                pl.BlockSpec(mask.shape, lambda h, f: (0, 0)),
                pl.BlockSpec((rows, HD), lambda h, f: (0, h)),
                picked(0),
                picked(1),
                picked(2),
                picked(0),
                picked(1),
                picked(2),
                pl.BlockSpec((count, HD), lambda h, f: (0, h)),
                pl.BlockSpec((count, HD), lambda h, f: (0, h)),
            ],
            out_specs=pl.BlockSpec((rows, HD), lambda h, f: (0, h)),
        ),
        out_shape=jax.ShapeDtypeStruct((rows, width), BF16),
        compiler_params=VMEM,
    )(
        frames, mask, query,
        cache_keys, cache_keys, cache_keys,
        cache_values, cache_values, cache_values,
        own_keys, own_values,
    )


def column(lead, tail, index):
    count = lead.shape[1] // HD
    ref, index = (lead, index) if index < count else (tail, index - count)
    return ref[:, index * HD : (index + 1) * HD]


def critic_kernel(q, lead, tail, out, lse):
    heads = q.shape[1] // HD
    for head in range(heads):
        here = slice(head * HD, (head + 1) * HD)
        scores = mm(q[:, here], column(lead, tail, head), 1, 1) * HD ** (-0.5)
        top = scores.max(axis=-1, keepdims=True)
        raised = jnp.exp(scores - top)
        total = raised.sum(axis=-1, keepdims=True)
        weights = (raised * (1.0 / total)).astype(BF16)
        out[:, here] = mm(weights, column(lead, tail, heads + head), 1, 0).astype(BF16)
        lse[:, here] = jnp.broadcast_to(top + jnp.log(total), (q.shape[0], HD))


def critic_attention(query, lead, tail):
    return pl.pallas_call(
        critic_kernel,
        out_shape=(
            jax.ShapeDtypeStruct(query.shape, BF16),
            jax.ShapeDtypeStruct(query.shape, F32),
        ),
        compiler_params=VMEM,
    )(query, lead, tail)


def query_kernel(q, lead, tail, lse, u, high, low, score, grad, sent):
    scale = HD ** (-0.5)
    width = q.shape[1]
    unit = u[...]
    stats = []
    for head, start in enumerate(range(0, width, HD)):
        here = slice(start, start + HD)
        keys = column(lead, tail, head)
        head_grad = (mm(unit, high[here, :], 1, 1) + mm(unit, low[here, :], 1, 1)).astype(BF16)
        logs = lse[:, start : start + 1]
        weights = jnp.exp(mm(q[:, here], keys, 1, 1) * scale - logs)
        slopes = mm(head_grad, column(lead, tail, width // HD + head), 1, 1)
        centred = jnp.sum(slopes * weights, axis=-1, keepdims=True)
        score_grad = (weights * (slopes - centred)).astype(BF16)
        grad[:, here] = (mm(score_grad, keys, 1, 0) * scale).astype(BF16)
        stats += [centred, logs]
    stats.append(score[...])
    lane = lax.broadcasted_iota(jnp.int32, (q.shape[0], HD), 1)
    table = jnp.zeros((q.shape[0], HD), F32)
    for i, stat in enumerate(stats):
        for j in range(3):
            term = stat.astype(BF16).astype(F32)
            table = jnp.where(lane == 3 * i + j, term, table)
            stat = stat - term
    sent[:, :HD] = unit
    sent[:, HD:] = table.astype(BF16)


def query_grads(query, lead, tail, lse, unit, high, low, score):
    rows, width = query.shape
    return pl.pallas_call(
        query_kernel,
        out_shape=(
            jax.ShapeDtypeStruct((rows, width), BF16),
            jax.ShapeDtypeStruct((rows, 2 * HD), BF16),
        ),
        compiler_params=VMEM,
    )(query, lead, tail, lse, unit, high, low, score)


def key_kernel(at, k, v, tail, sent, high, low, key_grad, value_grad, ordered_sent):
    scale = HD ** (-0.5)
    rows, width = k.shape
    y, z = at[0] // 4, at[0] % 4
    for dy in range(4):
        for dz in range(4):
            place = ((y + 4 - dy) % 4) * 4 + (z + 4 - dz) % 4
            block = (4 * dy + dz) * rows
            ordered_sent[block : block + rows, :] = sent[pl.ds(place, 1)][0]
    unit = ordered_sent[:, :HD]
    table = ordered_sent[:, HD:].astype(F32)

    def stat(i):
        return table[:, 3 * i : 3 * i + 1] + table[:, 3 * i + 1 : 3 * i + 2] + table[:, 3 * i + 2 : 3 * i + 3]

    first = tail.shape[1] - width
    for head, start in enumerate(range(0, width, HD)):
        here = slice(start, start + HD)
        queries = tail[:, first + start : first + start + HD]
        head_grad = (mm(unit, high[here, :], 1, 1) + mm(unit, low[here, :], 1, 1)).astype(BF16)
        weights = jnp.exp(mm(queries, k[:, here], 1, 1) * scale - stat(2 * head + 1))
        slopes = mm(head_grad, v[:, here], 1, 1)
        score_grad = (weights * (slopes - stat(2 * head))).astype(BF16)
        key_grad[:, here] = (mm(score_grad, queries, 0, 0) * scale).astype(BF16)
        value_grad[:, here] = mm(weights.astype(BF16), head_grad, 0, 0).astype(BF16)


def key_grads(at, keys, values, tail, sent, high, low):
    shape = jax.ShapeDtypeStruct(keys.shape, BF16)
    whole = pl.BlockSpec(memory_space=pltpu.VMEM)
    return pl.pallas_call(
        key_kernel,
        in_specs=[pl.BlockSpec(memory_space=pltpu.SMEM)] + [whole] * 6,
        out_shape=(shape, shape),
        scratch_shapes=[pltpu.VMEM((tail.shape[0], sent.shape[-1]), BF16)],
        compiler_params=VMEM,
    )(at, keys, values, tail, sent, high, low)


def split(value):
    high = lax.reduce_precision(value, 8, 7)
    return high.astype(BF16), (value - high).astype(BF16)


def normalised(row_block, gain_vector):
    lifted = row_block.astype(F32)
    inverse = lax.rsqrt(jnp.mean(lifted * lifted, axis=-1, keepdims=True) + EPS)
    return (lifted * inverse * gain_vector).astype(BF16), inverse


def times(a, b):
    return jnp.dot(a, b, preferred_element_type=F32).astype(BF16)


def unit_terms(units, head_out):
    active, back = jax.vjp(jax.nn.gelu, units)
    score = jnp.sum(active * head_out, axis=-1, keepdims=True)
    return score, back(jnp.broadcast_to(head_out, units.shape))[0].astype(BF16)


def pick_rows(real_bank, real_pick):
    chosen = jnp.zeros(real_bank.shape[1:], real_bank.dtype)
    for entry in range(real_bank.shape[0]):
        chosen = jnp.where((real_pick == entry)[:, None], real_bank[entry], chosen)
    return chosen


GEN, CRIT = (0,), (1,)


def local(
    new_rows, cache_keys, cache_values, cache_frames, real_bank, real_pick,
    attn_weights, out_weights, norm_gains, head_in, head_out,
):
    is_gen = lax.axis_index("grp") == 0
    seq_at, fsdp_at = lax.axis_index("seq"), lax.axis_index("fsdp")
    y, z, x, w = seq_at // 4, seq_at % 4, fsdp_at // 2, fsdp_at % 2
    rows, model = new_rows.shape
    cols = out_weights.shape[2]
    width = attn_weights.shape[3]
    tokens = rows * 16
    gains = norm_gains[0]
    start = fsdp_at * cols

    shard = jnp.concatenate([attn_weights[0, c] for c in range(3)], axis=1)
    weights = lax.all_gather(shard, "seq", axis=0, tiled=True)
    full_out = lax.all_gather(out_weights[0], "seq", axis=0, tiled=True)

    real_rows = pick_rows(real_bank, real_pick)
    first_rows = jnp.where(is_gen, new_rows, real_rows)
    first_normed, _ = normalised(first_rows, gains)
    first = times(first_normed, weights)
    first_q = first[:, :width]
    first_kv = ring4(ring4(first[:, width:], 1, (0, 1)), 0, (0, 1)).reshape(tokens, 2 * width)
    first_k, first_v = first_kv[:, :width], first_kv[:, width:]
    key_y = (y - jnp.arange(tokens) // (4 * rows)) % 4
    mask = jnp.broadcast_to((key_y // 2 <= y // 2).astype(F32)[None], (8, tokens))
    first_heads = lax.cond(
        is_gen,
        lambda a: generator_attention(*a),
        lambda a: critic_attention(a[2], a[5], a[6])[0],
        (cache_frames, mask, first_q, cache_keys, cache_values, first_k, first_v),
    )

    joint = jnp.dot(full_out, head_in, preferred_element_type=F32)
    first_all = spread(first_heads, "fsdp").transpose(1, 0, 2).reshape(rows, 8 * width)
    first_all = after(first_all, joint)
    first_cols = lax.dynamic_slice_in_dim(first_rows, start, cols, 1).astype(F32)
    generated = (first_cols + jnp.dot(first_all, full_out, preferred_element_type=F32)).astype(BF16)
    crossed = spread(across(generated, GEN), "fsdp")
    second_rows = crossed.transpose(1, 0, 2).reshape(rows, model)

    to_seq = first_all.reshape(rows, 4, 4, 192).transpose(1, 2, 0, 3)
    gen_heads = swap_seq(jnp.roll(to_seq, (-y, -z), (0, 1)), GEN).reshape(tokens, 192)

    high, low = split(lax.psum_scatter(joint, "fsdp", scatter_dimension=0, tiled=True))

    def units_of(row_cols, heads):
        part = jnp.dot(row_cols, head_in, preferred_element_type=F32)
        part = part + jnp.dot(heads, high, preferred_element_type=F32)
        return part + jnp.dot(heads, low, preferred_element_type=F32)

    real_cols = lax.dynamic_slice_in_dim(first_rows, start, cols, 1)

    second_normed, inverse = normalised(second_rows, gains)
    second = times(second_normed, weights)
    second_q, second_k, second_v = (second[:, c * width : (c + 1) * width] for c in range(3))
    cut = width - HD
    every_lead, every_tail = gather_seq(
        jnp.concatenate([second_k, second_v[:, :cut]], axis=1),
        jnp.concatenate([second_v[:, cut:], second_q], axis=1),
        CRIT,
    )
    second_heads, lse = critic_attention(second_q, every_lead, every_tail)
    second_cols = lax.dynamic_slice_in_dim(second_rows, start, cols, 1)
    units = jnp.stack([units_of(real_cols, after(first_heads, second_heads)), units_of(second_cols, second_heads)])
    units = after(jnp.sum(spread(units, "fsdp"), axis=0), gen_heads)
    real_score, real_unit = unit_terms(units[0], head_out)
    fake_score, fake_unit = unit_terms(units[1], head_out)
    query_grad, sent = query_grads(
        second_q, every_lead, every_tail, lse, fake_unit, high, low, real_score - fake_score
    )
    sent = spread(sent, "seq")
    at = jnp.reshape(seq_at, (1,)).astype(jnp.int32)
    key_grad, value_grad = key_grads(at, second_k, second_v, every_tail, sent, high, low)
    grads = jnp.concatenate([query_grad, key_grad, value_grad], axis=1)
    row_terms = jnp.einsum(
        "tk,bnk->btn", grads, weights.reshape(8, cols, 3 * width), preferred_element_type=F32
    )
    product = mm(second_heads, fake_unit, 0, 0) - mm(first_heads, real_unit, 0, 0)
    product = [product[i * HD : (i + 1) * HD] for i in range(width // HD)]
    product = jnp.concatenate(product, axis=1).astype(BF16)
    product = jnp.broadcast_to(product[None], (8,) + product.shape)
    joined = jnp.concatenate([row_terms.astype(BF16), product], axis=2)
    joined = lax.all_to_all(joined, "fsdp", 0, 0)
    row_grad = jnp.sum(joined[:, :, :cols].astype(F32), axis=0)
    gain_cols = lax.dynamic_slice_in_dim(gains, start, cols, 0)
    direction = mm(fake_unit, head_in, 1, 1)
    input_grad = (inverse * row_grad * gain_cols + direction).astype(BF16)

    product = [joined[:, :, i : i + HD] for i in range(cols, cols + width, HD)]
    product = lax.all_to_all(jnp.stack(product, axis=1).reshape(16, 192, HD), "seq", 0, 0)
    product_high, product_low = split(jnp.sum(product.astype(F32), axis=0))
    term_crit = mm(product_high, head_in, 1, 1) + mm(product_low, head_in, 1, 1)

    back = direct4(across(direct4(input_grad, 1, CRIT), CRIT), 0, GEN)
    back = back.reshape(tokens, cols)
    term_gen = mm(gen_heads, back, 0, 0)

    stats = sent[:, :, HD:].astype(F32)
    margin = jnp.sum(stats[:, :, 18:21]) / tokens
    margin_back = across(jnp.broadcast_to(margin, (8, HD)), CRIT)[0, 0]
    margin = jnp.where(is_gen, margin_back, margin)
    signed = jnp.where(is_gen, margin, -margin)
    factor = jnp.where(is_gen, -1.0, 1.0) * jax.nn.sigmoid(signed)
    grads = (jnp.where(is_gen, term_gen, term_crit) * factor).astype(BF16)
    losses = jax.nn.softplus(signed).astype(BF16)
    return (grads[None], losses[None])


def solution(mesh):
    placed = (
        P("seq", None),
        P(None, None, "fsdp"),
        P(None, None, "fsdp"),
        P(),
        P(None, "seq", None),
        P("seq"),
        P("grp", None, "seq", "fsdp"),
        P("grp", "seq", "fsdp"),
        P("grp", None),
        P("fsdp", None),
        P(),
    )
    return jax.shard_map(
        local,
        mesh=mesh,
        in_specs=placed,
        out_specs=(P("grp", "seq", "fsdp"), P("grp")),
        check_vma=False,
    )
```

```python
import jax
import jax.numpy as jnp
from jax import lax
from jax.experimental import pallas as pl
from jax.experimental.pallas import tpu as pltpu
from jax.sharding import PartitionSpec as P

HD = 128
STATS = 32
EPS = 1e-06
NEG = -1e30
AXES = ("grp", "seq", "fsdp")
VMEM = pltpu.CompilerParams(vmem_limit_bytes=50 * 2**20)
F32, BF16 = jnp.float32, jnp.bfloat16


def moved(value, step, groups=(0, 1), cross=False):
    dy, dz, dx, dw = step
    pairs = []
    for g in groups:
        for y in range(4):
            for z in range(4):
                for x in range(4):
                    for w in range(2):
                        there = 1 - g if cross else g
                        source = g * 128 + (4 * y + z) * 8 + 2 * x + w
                        target = (
                            there * 128
                            + (4 * ((y + dy) % 4) + (z + dz) % 4) * 8
                            + 2 * ((x + dx) % 4)
                            + (w + dw) % 2
                        )
                        pairs.append((source, target))
    return lax.ppermute(value, AXES, pairs)


def along(axis, k):
    step = [0, 0, 0, 0]
    step[axis] = k
    return tuple(step)


def ring4(value, axis, groups):
    one = moved(value, along(axis, 1), groups)
    three = moved(value, along(axis, -1), groups)
    cut = value.ndim - 2
    half = value.shape[cut] // 2
    low = lax.slice_in_dim(one, 0, half, axis=cut)
    high = lax.slice_in_dim(three, half, 2 * half, axis=cut)
    low = moved(low, along(axis, 1), groups)
    high = moved(high, along(axis, -1), groups)
    return jnp.stack([value, one, jnp.concatenate([low, high], axis=cut), three])


def direct4(value, axis, groups):
    return jnp.stack([value] + [moved(value, along(axis, k), groups) for k in (1, 2, 3)])


def gather_seq(lead, tail, groups):
    lead, tail = direct4(lead, 1, groups), direct4(tail, 0, groups)
    lead = direct4(lead, 0, groups)
    tail = jnp.stack([tail] + [moved(tail, along(1, k), groups) for k in (1, 2, 3)], axis=1)
    return [part.reshape((-1, part.shape[-1])) for part in (lead, tail)]


def spread(value, axis):
    count = lax.axis_size(axis)
    return lax.all_to_all(jnp.broadcast_to(value[None], (count,) + value.shape), axis, 0, 0)


def swap_seq(blocks, groups):
    rows = [blocks[0]] + [moved(blocks[k], along(0, k), groups) for k in (1, 2, 3)]
    rows = jnp.stack(rows)
    cols = [rows[:, 0]] + [moved(rows[:, k], along(1, k), groups) for k in (1, 2, 3)]
    return jnp.stack(cols, axis=1)


def across(value, groups):
    return moved(value, (0, 0, 0, 0), groups, cross=True)


def after(value, other):
    first = other[(slice(0, 1),) * other.ndim].reshape(())
    return value + (first.astype(F32) * 0.0).astype(value.dtype)


def mm(a, b, ca, cb):
    return lax.dot_general(a, b, (((ca,), (cb,)), ((), ())), preferred_element_type=F32)


def generator_kernel(frames, mask, q, k0, k1, k2, v0, v1, v2, own_k, own_v, out):
    scale = HD ** (-0.5)
    query = q[...]
    parts = [mm(query, k[0], 1, 1) * scale for k in (k0, k1, k2)]
    own = mm(query, own_k[...], 1, 1) * scale
    parts.append(jnp.where(mask[0:1, :] > 0.5, own, NEG))
    top = parts[0].max(axis=-1, keepdims=True)
    for part in parts[1:]:
        top = jnp.maximum(top, part.max(axis=-1, keepdims=True))
    parts = [jnp.exp(part - top) for part in parts]
    total = sum(part.sum(axis=-1, keepdims=True) for part in parts)
    inverse = 1.0 / total
    values = [v0[0], v1[0], v2[0], own_v[...]]
    result = jnp.zeros(out.shape, F32)
    for part, value in zip(parts, values):
        result = result + mm((part * inverse).astype(BF16), value, 1, 0)
    out[...] = result.astype(BF16)


def generator_attention(frames, mask, query, cache_keys, cache_values, own_keys, own_values):
    rows, width = query.shape
    heads = width // HD
    count, length = own_keys.shape[0], cache_keys.shape[1]

    def picked(i):
        return pl.BlockSpec((1, length, HD), lambda h, f: (f[i], 0, h))

    return pl.pallas_call(
        generator_kernel,
        grid_spec=pltpu.PrefetchScalarGridSpec(
            num_scalar_prefetch=1,
            grid=(heads,),
            in_specs=[
                pl.BlockSpec(mask.shape, lambda h, f: (0, 0)),
                pl.BlockSpec((rows, HD), lambda h, f: (0, h)),
                picked(0),
                picked(1),
                picked(2),
                picked(0),
                picked(1),
                picked(2),
                pl.BlockSpec((count, HD), lambda h, f: (0, h)),
                pl.BlockSpec((count, HD), lambda h, f: (0, h)),
            ],
            out_specs=pl.BlockSpec((rows, HD), lambda h, f: (0, h)),
        ),
        out_shape=jax.ShapeDtypeStruct((rows, width), BF16),
        compiler_params=VMEM,
    )(
        frames, mask, query,
        cache_keys, cache_keys, cache_keys,
        cache_values, cache_values, cache_values,
        own_keys, own_values,
    )


def column(lead, tail, index):
    count = lead.shape[1] // HD
    ref, index = (lead, index) if index < count else (tail, index - count)
    return ref[:, index * HD : (index + 1) * HD]


def critic_kernel(q, lead, tail, out, lse):
    heads = q.shape[1] // HD
    for head in range(heads):
        here = slice(head * HD, (head + 1) * HD)
        scores = mm(q[:, here], column(lead, tail, head), 1, 1) * HD ** (-0.5)
        top = scores.max(axis=-1, keepdims=True)
        raised = jnp.exp(scores - top)
        total = raised.sum(axis=-1, keepdims=True)
        weights = (raised * (1.0 / total)).astype(BF16)
        out[:, here] = mm(weights, column(lead, tail, heads + head), 1, 0).astype(BF16)
        lse[:, here] = jnp.broadcast_to(top + jnp.log(total), (q.shape[0], HD))


def critic_attention(query, lead, tail):
    return pl.pallas_call(
        critic_kernel,
        out_shape=(
            jax.ShapeDtypeStruct(query.shape, BF16),
            jax.ShapeDtypeStruct(query.shape, F32),
        ),
        compiler_params=VMEM,
    )(query, lead, tail)


def query_kernel(q, lead, tail, lse, u, high, low, score, grad, sent):
    scale = HD ** (-0.5)
    width = q.shape[1]
    unit = u[...]
    stats = []
    for head, start in enumerate(range(0, width, HD)):
        here = slice(start, start + HD)
        keys = column(lead, tail, head)
        head_grad = (mm(unit, high[here, :], 1, 1) + mm(unit, low[here, :], 1, 1)).astype(BF16)
        logs = lse[:, start : start + 1]
        weights = jnp.exp(mm(q[:, here], keys, 1, 1) * scale - logs)
        slopes = mm(head_grad, column(lead, tail, width // HD + head), 1, 1)
        centred = jnp.sum(slopes * weights, axis=-1, keepdims=True)
        score_grad = (weights * (slopes - centred)).astype(BF16)
        grad[:, here] = (mm(score_grad, keys, 1, 0) * scale).astype(BF16)
        stats += [centred, logs]
    stats.append(score[...])
    lane = lax.broadcasted_iota(jnp.int32, (q.shape[0], HD), 1)
    table = jnp.zeros((q.shape[0], HD), F32)
    for i, stat in enumerate(stats):
        for j in range(3):
            term = stat.astype(BF16).astype(F32)
            table = jnp.where(lane == 3 * i + j, term, table)
            stat = stat - term
    sent[:HD, :] = unit
    sent[HD:, :] = table.T[:STATS, :].astype(BF16)


def query_grads(query, lead, tail, lse, unit, high, low, score):
    rows, width = query.shape
    return pl.pallas_call(
        query_kernel,
        out_shape=(
            jax.ShapeDtypeStruct((rows, width), BF16),
            jax.ShapeDtypeStruct((rows + STATS, HD), BF16),
        ),
        compiler_params=VMEM,
    )(query, lead, tail, lse, unit, high, low, score)


def key_kernel(at, k, v, tail, sent, high, low, key_grad, value_grad, units, table_of):
    scale = HD ** (-0.5)
    rows, width = k.shape
    y, z = at[0] // 4, at[0] % 4
    for dy in range(4):
        for dz in range(4):
            place = ((y + 4 - dy) % 4) * 4 + (z + 4 - dz) % 4
            block = (4 * dy + dz) * rows
            came = sent[pl.ds(place, 1)][0]
            units[block : block + rows, :] = came[:rows, :]
            table_of[block : block + rows, :] = came[rows:, :].astype(F32).T
    unit = units[...]
    table = table_of[...]

    def stat(i):
        return table[:, 3 * i : 3 * i + 1] + table[:, 3 * i + 1 : 3 * i + 2] + table[:, 3 * i + 2 : 3 * i + 3]

    first = tail.shape[1] - width
    for head, start in enumerate(range(0, width, HD)):
        here = slice(start, start + HD)
        queries = tail[:, first + start : first + start + HD]
        head_grad = (mm(unit, high[here, :], 1, 1) + mm(unit, low[here, :], 1, 1)).astype(BF16)
        weights = jnp.exp(mm(queries, k[:, here], 1, 1) * scale - stat(2 * head + 1))
        slopes = mm(head_grad, v[:, here], 1, 1)
        score_grad = (weights * (slopes - stat(2 * head))).astype(BF16)
        key_grad[:, here] = (mm(score_grad, queries, 0, 0) * scale).astype(BF16)
        value_grad[:, here] = mm(weights.astype(BF16), head_grad, 0, 0).astype(BF16)


def key_grads(at, keys, values, tail, sent, high, low):
    shape = jax.ShapeDtypeStruct(keys.shape, BF16)
    whole = pl.BlockSpec(memory_space=pltpu.VMEM)
    return pl.pallas_call(
        key_kernel,
        in_specs=[pl.BlockSpec(memory_space=pltpu.SMEM)] + [whole] * 6,
        out_shape=(shape, shape),
        scratch_shapes=[
            pltpu.VMEM((tail.shape[0], HD), BF16),
            pltpu.VMEM((tail.shape[0], STATS), F32),
        ],
        compiler_params=VMEM,
    )(at, keys, values, tail, sent, high, low)


def split(value):
    high = lax.reduce_precision(value, 8, 7)
    return high.astype(BF16), (value - high).astype(BF16)


def normalised(row_block, gain_vector):
    lifted = row_block.astype(F32)
    inverse = lax.rsqrt(jnp.mean(lifted * lifted, axis=-1, keepdims=True) + EPS)
    return (lifted * inverse * gain_vector).astype(BF16), inverse


def times(a, b):
    return jnp.dot(a, b, preferred_element_type=F32).astype(BF16)


def unit_terms(units, head_out):
    active, back = jax.vjp(jax.nn.gelu, units)
    score = jnp.sum(active * head_out, axis=-1, keepdims=True)
    return score, back(jnp.broadcast_to(head_out, units.shape))[0].astype(BF16)


def pick_rows(real_bank, real_pick):
    chosen = jnp.zeros(real_bank.shape[1:], real_bank.dtype)
    for entry in range(real_bank.shape[0]):
        chosen = jnp.where((real_pick == entry)[:, None], real_bank[entry], chosen)
    return chosen


GEN, CRIT = (0,), (1,)


def local(
    new_rows, cache_keys, cache_values, cache_frames, real_bank, real_pick,
    attn_weights, out_weights, norm_gains, head_in, head_out,
):
    is_gen = lax.axis_index("grp") == 0
    seq_at, fsdp_at = lax.axis_index("seq"), lax.axis_index("fsdp")
    y, z, x, w = seq_at // 4, seq_at % 4, fsdp_at // 2, fsdp_at % 2
    rows, model = new_rows.shape
    cols = out_weights.shape[2]
    width = attn_weights.shape[3]
    tokens = rows * 16
    gains = norm_gains[0]
    start = fsdp_at * cols

    shard = jnp.concatenate([attn_weights[0, c] for c in range(3)], axis=1)
    weights = lax.all_gather(shard, "seq", axis=0, tiled=True)
    full_out = lax.all_gather(out_weights[0], "seq", axis=0, tiled=True)

    real_rows = pick_rows(real_bank, real_pick)
    first_rows = jnp.where(is_gen, new_rows, real_rows)
    first_normed, _ = normalised(first_rows, gains)
    first = times(first_normed, weights)
    first_q = first[:, :width]
    first_kv = ring4(ring4(first[:, width:], 1, (0, 1)), 0, (0, 1)).reshape(tokens, 2 * width)
    first_k, first_v = first_kv[:, :width], first_kv[:, width:]
    key_y = (y - jnp.arange(tokens) // (4 * rows)) % 4
    mask = jnp.broadcast_to((key_y // 2 <= y // 2).astype(F32)[None], (8, tokens))
    first_heads = lax.cond(
        is_gen,
        lambda a: generator_attention(*a),
        lambda a: critic_attention(a[2], a[5], a[6])[0],
        (cache_frames, mask, first_q, cache_keys, cache_values, first_k, first_v),
    )

    joint = jnp.dot(full_out, head_in, preferred_element_type=F32)
    first_all = spread(first_heads, "fsdp").transpose(1, 0, 2).reshape(rows, 8 * width)
    first_all = after(first_all, joint)
    first_cols = lax.dynamic_slice_in_dim(first_rows, start, cols, 1).astype(F32)
    generated = (first_cols + jnp.dot(first_all, full_out, preferred_element_type=F32)).astype(BF16)
    crossed = spread(across(generated, GEN), "fsdp")
    second_rows = crossed.transpose(1, 0, 2).reshape(rows, model)

    to_seq = first_all.reshape(rows, 4, 4, 192).transpose(1, 2, 0, 3)
    gen_heads = swap_seq(jnp.roll(to_seq, (-y, -z), (0, 1)), GEN).reshape(tokens, 192)

    high, low = split(lax.psum_scatter(joint, "fsdp", scatter_dimension=0, tiled=True))

    def units_of(row_cols, heads):
        part = jnp.dot(row_cols, head_in, preferred_element_type=F32)
        part = part + jnp.dot(heads, high, preferred_element_type=F32)
        return part + jnp.dot(heads, low, preferred_element_type=F32)

    real_cols = lax.dynamic_slice_in_dim(first_rows, start, cols, 1)

    second_normed, inverse = normalised(second_rows, gains)
    second = times(second_normed, weights)
    second_q, second_k, second_v = (second[:, c * width : (c + 1) * width] for c in range(3))
    cut = width - HD
    every_lead, every_tail = gather_seq(
        jnp.concatenate([second_k, second_v[:, :cut]], axis=1),
        jnp.concatenate([second_v[:, cut:], second_q], axis=1),
        CRIT,
    )
    second_heads, lse = critic_attention(second_q, every_lead, every_tail)
    second_cols = lax.dynamic_slice_in_dim(second_rows, start, cols, 1)
    units = jnp.stack([units_of(real_cols, after(first_heads, second_heads)), units_of(second_cols, second_heads)])
    units = spread(units.astype(BF16), "fsdp").astype(F32)
    units = after(jnp.sum(units, axis=0), gen_heads)
    real_score, real_unit = unit_terms(units[0], head_out)
    fake_score, fake_unit = unit_terms(units[1], head_out)
    query_grad, sent = query_grads(
        second_q, every_lead, every_tail, lse, fake_unit, high, low, real_score - fake_score
    )
    sent = spread(sent, "seq")
    at = jnp.reshape(seq_at, (1,)).astype(jnp.int32)
    key_grad, value_grad = key_grads(at, second_k, second_v, every_tail, sent, high, low)
    grads = jnp.concatenate([query_grad, key_grad, value_grad], axis=1)
    row_terms = jnp.einsum(
        "tk,bnk->btn", grads, weights.reshape(8, cols, 3 * width), preferred_element_type=F32
    )
    row_terms = lax.all_to_all(row_terms.astype(BF16), "fsdp", 0, 0)
    row_grad = jnp.sum(row_terms.astype(F32), axis=0)
    gain_cols = lax.dynamic_slice_in_dim(gains, start, cols, 0)
    direction = mm(fake_unit, head_in, 1, 1)
    input_grad = (inverse * row_grad * gain_cols + direction).astype(BF16)

    product = mm(second_heads, fake_unit, 0, 0) - mm(first_heads, real_unit, 0, 0)
    product = spread(product.astype(BF16), "fsdp").reshape(16, 192, -1)
    product = lax.all_to_all(product, "seq", 0, 0)
    product_high, product_low = split(jnp.sum(product.astype(F32), axis=0))
    term_crit = mm(product_high, head_in, 1, 1) + mm(product_low, head_in, 1, 1)

    back = direct4(across(direct4(input_grad, 1, CRIT), CRIT), 0, GEN)
    back = back.reshape(tokens, cols)
    term_gen = mm(gen_heads, back, 0, 0)

    stats = sent[:, rows:, :].astype(F32)
    margin = jnp.sum(stats[:, 18:21, :]) / tokens
    margin_back = across(jnp.broadcast_to(margin, (8, HD)), CRIT)[0, 0]
    margin = jnp.where(is_gen, margin_back, margin)
    signed = jnp.where(is_gen, margin, -margin)
    factor = jnp.where(is_gen, -1.0, 1.0) * jax.nn.sigmoid(signed)
    grads = (jnp.where(is_gen, term_gen, term_crit) * factor).astype(BF16)
    losses = jax.nn.softplus(signed).astype(BF16)
    return (grads[None], losses[None])


def solution(mesh):
    placed = (
        P("seq", None),
        P(None, None, "fsdp"),
        P(None, None, "fsdp"),
        P(),
        P(None, "seq", None),
        P("seq"),
        P("grp", None, "seq", "fsdp"),
        P("grp", "seq", "fsdp"),
        P("grp", None),
        P("fsdp", None),
        P(),
    )
    return jax.shard_map(
        local,
        mesh=mesh,
        in_specs=placed,
        out_specs=(P("grp", "seq", "fsdp"), P("grp")),
        check_vma=False,
    )
```
